512 devices in a mesh: blk: 128 (over x, y_hi, z, core), pair: 4 (over y_lo).
Axes of the slice: x: 4, y: 8 (y_hi: 2, y_lo: 4; y = y_hi * 4 + y_lo), z: 8, core: 2. Of those that a mesh axis runs over, the one named last changes fastest.
Arguments:
- half_blocks: bfloat16 [16384, 32, 256], P('blk', 'pair'), may hold values from -6 to 6
- row_target: int32 [16384], P('blk'), may hold values from 0 to 16383, as said below
- vir_coeff: bfloat16 [256, 128], replicated, may hold values from -0.375 to 0.375
- occ_energy: float32 [32], replicated, may hold values from -2 to -0.3
- vir_energy: float32 [128], replicated, may hold values from 0.1 to 3
- freq_pick: int32 [6], replicated, may hold values from 0 to 31
Outputs:
- response: float32 [6, 16384, 1024], P(None, 'blk', 'pair')
The draws below stay inside these ranges and needn't reach their ends.
Inputs may be any that keep to these rules, and one draw needn't show every extreme that they name: row_target is a permutation of the auxiliary functions. The rows of one device go at most 2 to the block of 128 functions of any one owner; every device sends exactly 2 rows to some owner, and every owner receives exactly 2 rows from some device. All devices send the same counts of rows, to owners paired in different ways.
All inputs are finite; a program needn't handle non-finite values.
Results may differ from the reference program's by a relative error of at most 0.0024.
Values may be sent and summed in bfloat16 or wider, within the bound.
A program may use at most 64 MiB of HBM per device.

```python
import math
import jax
import jax.numpy as jnp
from jax import lax

NBAS = 256
NVIR = 128
ROWS = 128
NFREQ = 6
STOPS = 8
GRID = 32
CAP = 2
NAUX = 16384
NOCC = 32


def draw_row_target(key, part):
    count = NAUX // ROWS
    shuffled = jax.random.permutation(jax.random.fold_in(key, 11), CAP * count)
    position = jnp.argsort(shuffled).astype(jnp.int32)
    busiest = jax.random.randint(jax.random.fold_in(key, 12), (), 0, count)
    slot_ids = jnp.arange(CAP * count, dtype=jnp.int32)
    priority = jnp.where(slot_ids // CAP == busiest, -1, position)
    chosen = jnp.argsort(priority)[:ROWS].astype(jnp.int32)
    offsets = jnp.sort(chosen // CAP)
    owner_perm = jax.random.permutation(jax.random.fold_in(key, 13), count)
    source_perm = jax.random.permutation(jax.random.fold_in(key, 14), count)
    source = jnp.arange(count, dtype=jnp.int32)[:, None]
    owners = owner_perm[(source_perm[source] + offsets[None, :]) % count]
    slot_perm = jax.vmap(lambda subkey: jax.random.permutation(subkey, ROWS))(jax.random.split(jax.random.fold_in(key, 15), count))
    landing = slot_perm[owners, jnp.arange(ROWS, dtype=jnp.int32)[None, :]]
    target = owners * ROWS + landing
    shuffle = jax.vmap(lambda subkey: jax.random.permutation(subkey, ROWS))(jax.random.split(jax.random.fold_in(key, 16), count))
    placed = jnp.zeros((count, ROWS), jnp.int32).at[source, shuffle].set(target.astype(jnp.int32))
    return placed.reshape(NAUX).astype(jnp.int32)


def place_ends(array, key, least, largest):
    dims = array.shape
    spot = [jax.random.randint(jax.random.fold_in(key, axis), (), 0, dims[axis]) for axis in range(len(dims))]
    array = array.at[tuple(spot)].set(least)
    longest = dims.index(max(dims))
    spot[longest] = (spot[longest] + 1) % dims[longest]
    return array.at[tuple(spot)].set(largest)


def shard_levels(key, dims, shards, smallest, top_value):
    def one(dim, parts):
        steps = jax.random.uniform(jax.random.fold_in(jax.random.fold_in(key, 6), dim), (parts,), jnp.float32, smallest / len(shards), top_value / len(shards))
        return jnp.repeat(jnp.exp(steps), dims[dim] // parts).reshape((-1,) + (1,) * (len(dims) - dim - 1))

    level = one(*shards[0])
    for cut in shards[1:]:
        level = level * one(*cut)
    return level


def gaussian(key, extent, deviation, reach, shards=(), kind=jnp.bfloat16):
    level = shard_levels(key, extent, shards, -0.22, 0.18) if shards else 1.0
    values = jax.random.normal(key, extent, jnp.float32) * deviation * level
    return jnp.minimum(jnp.maximum(values, -reach), reach).astype(kind)


def setup_inputs(seed: int = 0) -> dict:
    arg_keys = jax.random.split(jax.random.key(seed), 7)
    half_blocks = gaussian(arg_keys[0], (NAUX, NOCC, NBAS), 1.0, 6.0, ((0, 128), (1, 4)))
    row_target = draw_row_target(jax.random.fold_in(arg_keys[6], 71), 0)
    vir_coeff = gaussian(arg_keys[2], (NBAS, NVIR), NBAS ** -0.5, 0.375)
    occ_energy = jnp.clip(jax.random.uniform(arg_keys[3], (NOCC,), jnp.float32, -2.0, -0.3), -2.0, -0.3)
    vir_energy = jnp.clip(jax.random.uniform(arg_keys[4], (NVIR,), jnp.float32, 0.1, 3.0), 0.1, 3.0)
    freq_pick = place_ends(jax.random.randint(arg_keys[5], (NFREQ,), 0, GRID), jax.random.fold_in(arg_keys[5], 1), 0, GRID - 1).astype(jnp.int32)
    return {"half_blocks": half_blocks, "row_target": row_target, "vir_coeff": vir_coeff, "occ_energy": occ_energy, "vir_energy": vir_energy, "freq_pick": freq_pick}


def response_factor(occ_values, vir_values, frequency):
    energy_gap = vir_values[None, :] - occ_values[:, None]
    factor = 2.0 * energy_gap[None] / (energy_gap[None] * energy_gap[None] + frequency[:, None, None] * frequency[:, None, None])
    return factor.reshape(frequency.shape[0], -1)

def reference(half_blocks, row_target, vir_coeff, occ_energy, vir_energy, freq_pick):
    aux_count, occ_count, basis = half_blocks.shape
    virtual = vir_coeff.shape[1]
    placed = jnp.zeros_like(half_blocks).at[row_target].set(half_blocks)
    vir_blocks = jnp.dot(placed.reshape(aux_count * occ_count, basis), vir_coeff, preferred_element_type=jnp.float32)
    vir_blocks = vir_blocks.astype(jnp.bfloat16).reshape(aux_count, occ_count * virtual)
    frequency = 0.5 * jnp.tan(jnp.pi * (freq_pick.astype(jnp.float32) + 0.5) / (2.0 * GRID))
    factor = response_factor(occ_energy, vir_energy, frequency)
    block_count = aux_count // ROWS
    lowest = STOPS // 2 - 1
    scaling = 1.0 / math.sqrt(occ_count * virtual)
    grouped = vir_blocks.reshape(block_count, ROWS, occ_count * virtual)

    def one_block(block_id):
        row_block = lax.dynamic_slice_in_dim(vir_blocks, block_id * ROWS, ROWS, 0)
        weighted = (row_block.astype(jnp.float32)[None] * factor[:, None, :]).astype(jnp.bfloat16)
        partner_ids = ((block_id + jnp.arange(STOPS, dtype=jnp.int32) - lowest) % block_count).astype(jnp.int32)
        partners = jnp.take(grouped, partner_ids, axis=0).reshape(STOPS * ROWS, occ_count * virtual)
        tiles = lax.dot_general(weighted.reshape(NFREQ * ROWS, -1).astype(jnp.float32), partners.astype(jnp.float32), (((1,), (1,)), ((), ())), precision=lax.Precision.HIGHEST)
        return tiles.reshape(NFREQ, ROWS, STOPS * ROWS) * scaling
    result = lax.map(one_block, jnp.arange(block_count, dtype=jnp.int32))
    return jnp.transpose(result, (1, 0, 2, 3)).reshape(NFREQ, aux_count, STOPS * ROWS)
```

```python
import functools

import jax
import jax.numpy as jnp
from jax import lax
from jax.experimental import pallas as pl
from jax.experimental.pallas import tpu as pltpu
from jax.sharding import PartitionSpec as P

MESH = pl.DeviceIdType.MESH
GRID = 32
STEPS = 8


def route_kernel(chips, depth, ids_ref, out_ref, got_ref, all_ids_ref, staged, arrived, ids, pair_sem, sems):
    blk, pair = lax.axis_index("blk"), lax.axis_index("pair")
    chip, core = blk // 2, lax.rem(blk, 2)
    upper, low = chip // depth, lax.rem(chip, depth)
    uppers = chips // depth
    sibling = (chip * 2 + 1 - core, pair)

    def same_core(other):
        return (other * 2 + core, pair)

    barrier = pltpu.get_barrier_semaphore()
    pl.semaphore_signal(barrier, inc=1, device_id=sibling, device_id_type=MESH)

    def greet(i, carry):
        pl.semaphore_signal(
            barrier, inc=1, device_id=same_core(lax.rem(chip + i, chips)), device_id_type=MESH
        )
        return carry

    lax.fori_loop(1, chips, greet, 0)
    pl.semaphore_wait(barrier, chips)

    ids[upper, low, core] = ids_ref[...]
    swap_ids = pltpu.make_async_remote_copy(
        ids.at[upper, low, core],
        ids.at[upper, low, core],
        pair_sem.at[0],
        pair_sem.at[1],
        device_id=sibling,
        device_id_type=MESH,
    )
    swap_ids.start()
    swap = pltpu.make_async_remote_copy(
        out_ref.at[1 - core],
        staged.at[:, core],
        pair_sem.at[2],
        pair_sem.at[3],
        device_id=sibling,
        device_id_type=MESH,
    )
    swap.start()
    staged[:, core] = out_ref[core]
    swap_ids.wait()
    for i in range(1, depth):
        pltpu.make_async_remote_copy(
            ids.at[upper, low],
            ids.at[upper, low],
            sems.at[0],
            sems.at[1],
            device_id=same_core(upper * depth + lax.rem(low + i, depth)),
            device_id_type=MESH,
        ).start()
    swap.wait()

    def send(i, carry):
        other = lax.rem(chip + i * 27, chips)
        pltpu.make_async_remote_copy(
            staged.at[other],
            arrived.at[chip],
            sems.at[2],
            sems.at[3],
            device_id=same_core(other),
            device_id_type=MESH,
        ).start()
        return carry

    lax.fori_loop(1, chips, send, 0)
    arrived[chip] = staged[chip]
    low_part = ids.at[0, pl.ds(0, depth - 1)]
    pltpu.make_async_remote_copy(
        low_part, low_part, sems.at[0], sems.at[1], device_id=sibling, device_id_type=MESH
    ).wait()
    for i in range(1, uppers):
        pltpu.make_async_remote_copy(
            ids.at[upper],
            ids.at[upper],
            sems.at[4],
            sems.at[5],
            device_id=same_core(lax.rem(upper + i, uppers) * depth + low),
            device_id_type=MESH,
        ).start()
    upper_part = ids.at[pl.ds(0, uppers - 1)]
    pltpu.make_async_remote_copy(
        upper_part, upper_part, sems.at[4], sems.at[5], device_id=sibling, device_id_type=MESH
    ).wait()
    all_ids_ref[...] = ids[...]
    most = arrived.at[pl.ds(0, chips - 1)]
    pltpu.make_async_remote_copy(
        most, most, sems.at[2], sems.at[3], device_id=sibling, device_id_type=MESH
    ).wait()
    got_ref[...] = arrived[...]


def band_kernel(
    chips, own_ref, factor_ref, result_ref, halo, weighted, partial, outbox, inbox,
    halo_send, halo_recv, core_send, core_recv, part_send, part_recv
):
    blk, pair = lax.axis_index("blk"), lax.axis_index("pair")
    pairs = 4
    chip, core = blk // 2, lax.rem(blk, 2)
    above = (lax.rem(chip + 1, chips) * 2 + core, pair)
    below = (lax.rem(chip + chips - 1, chips) * 2 + core, pair)
    sibling = (chip * 2 + 1 - core, pair)
    freqs = factor_ref.shape[0]
    rows = own_ref.shape[0]

    barrier = pltpu.get_barrier_semaphore()
    for other in (above, below, sibling):
        pl.semaphore_signal(barrier, inc=1, device_id=other, device_id_type=MESH)
    for i in range(1, pairs):
        pl.semaphore_signal(
            barrier, inc=1, device_id=(blk, lax.rem(pair + i, pairs)), device_id_type=MESH
        )
    pl.semaphore_wait(barrier, 3 + pairs - 1)

    def link(source, slot, lane, other):
        return pltpu.make_async_remote_copy(
            source, halo.at[slot], halo_send.at[lane], halo_recv.at[lane], device_id=other, device_id_type=MESH
        )

    def across(source, slot, lane):
        return pltpu.make_async_remote_copy(
            source, halo.at[slot], core_send.at[lane], core_recv.at[lane], device_id=sibling, device_id_type=MESH
        )

    up = link(own_ref, 1 + core, 0, above)
    down = link(own_ref, 5 + core, 1, below)
    beside = across(own_ref, 3 + core, 0)
    down.start()
    up.start()
    beside.start()

    for k in range(freqs):
        weighted[pl.ds(k * rows, rows)] = (
            own_ref[...].astype(jnp.float32) * factor_ref[pl.ds(k, 1)]
        ).astype(jnp.bfloat16)

    def send_part(step, stop):
        return pltpu.make_async_remote_copy(
            outbox.at[step],
            inbox.at[pair, lax.rem(stop, 2)],
            part_send.at[step],
            part_recv.at[pair, lax.rem(stop, 2)],
            device_id=(blk, stop // 2),
            device_id_type=MESH,
        )

    def tile(step, stop, block):
        value = lax.dot_general(
            weighted[...], block, (((1,), (1,)), ((), ())), preferred_element_type=jnp.float32
        )

        @pl.when(stop // 2 == pair)
        def _():
            partial[lax.rem(stop, 2)] = value

        @pl.when(stop // 2 != pair)
        def _():
            outbox[step] = value.astype(jnp.bfloat16)
            send_part(step, stop).start()

    stops = (3, 4 - 2 * core, 1, 5, 2 - 2 * core, 6 - 2 * core, 6 * core, 7)
    tile(0, stops[0], own_ref[...])
    beside.wait_recv()
    tile(1, stops[1], halo[4 - core])
    down.wait_recv()
    down2 = link(halo.at[5 + core], 7 + core, 2, below)
    down2.start()
    cross_down = across(halo.at[5 + core], 5 + core, 1)
    cross_down.start()
    up.wait_recv()
    up2 = link(halo.at[2], 0, 3, above)

    @pl.when(core == 1)
    def _():
        up2.start()

    cross_up = across(halo.at[1 + core], 1 + core, 2)
    cross_up.start()
    tile(2, stops[2], halo[1 + core])
    tile(3, stops[3], halo[5 + core])
    cross_up.wait_recv()
    tile(4, stops[4], halo[2 - core])
    cross_down.wait_recv()
    tile(5, stops[5], halo[6 - core])
    last = across(halo.at[7 - 7 * core], 7 - 7 * core, 3)
    down2.wait_recv()

    @pl.when(core == 0)
    def _():
        last.start()

    tile(7, stops[7], halo[7 + core])

    @pl.when(core == 1)
    def _():
        up2.wait_recv()
        last.start()

    last.wait_recv()
    tile(6, stops[6], halo[7 * core])

    for copy in (up, down, down2, beside, cross_up, cross_down, last):
        copy.wait_send()

    @pl.when(core == 1)
    def _():
        up2.wait_send()

    for i in range(1, pairs):
        other = lax.rem(pair + i, pairs)
        for half in range(2):
            pltpu.make_async_remote_copy(
                outbox.at[0],
                inbox.at[other, half],
                part_send.at[0],
                part_recv.at[other, half],
                device_id=(blk, other),
                device_id_type=MESH,
            ).wait_recv()
    for step in range(STEPS):

        @pl.when(stops[step] // 2 != pair)
        def _():
            send_part(step, stops[step]).wait_send()

    scaling = 1.0 / 64.0
    for half in range(2):
        total = partial[half]
        for i in range(1, pairs):
            total = total + inbox[lax.rem(pair + i, pairs), half].astype(jnp.float32)
        result_ref[:, :, half * rows : (half + 1) * rows] = (total * scaling).reshape(freqs, rows, rows)


def response_factor(occ_values, vir_values, frequency):
    gap = vir_values[None, :] - occ_values[:, None]
    factor = 2.0 * gap[None] / (gap[None] * gap[None] + (frequency * frequency)[:, None, None])
    return factor.reshape(frequency.shape[0], -1)


def shards(half_blocks, row_target, vir_coeff, occ_energy, vir_energy, freq_pick):
    devices = lax.axis_size("blk")
    chips = devices // 2
    rows, occ, basis = half_blocks.shape
    virtual = vir_coeff.shape[1]
    width = occ * virtual
    freqs = freq_pick.shape[0]
    row_ids = jnp.arange(rows, dtype=jnp.int32)

    virt = jnp.dot(
        half_blocks.reshape(rows * occ, basis), vir_coeff, preferred_element_type=jnp.float32
    ).astype(jnp.bfloat16)
    owner = row_target // rows
    alike = owner[:, None] == owner[None, :]
    rank = jnp.sum((alike & (row_ids[None, :] < row_ids[:, None])).astype(jnp.int32), axis=1)
    slot = lax.rem(owner, 2) * devices + (owner // 2) * 2 + rank
    slots = jnp.arange(2 * devices, dtype=jnp.int32)
    pick = (slots[:, None] == slot[None, :]).astype(jnp.bfloat16)
    outgoing = jnp.dot(pick, virt.reshape(rows, width), preferred_element_type=jnp.float32)
    outgoing = outgoing.astype(jnp.bfloat16).reshape(2, chips, 2 * occ, virtual)

    depth = 8
    vmem = pl.BlockSpec(memory_space=pltpu.VMEM)
    got, ids = pl.pallas_call(
        functools.partial(route_kernel, chips, depth),
        out_shape=(
            jax.ShapeDtypeStruct((chips, 2, 2 * occ, virtual), jnp.bfloat16),
            jax.ShapeDtypeStruct((chips // depth, depth, 2, 1, rows), jnp.int32),
        ),
        in_specs=[vmem, vmem],
        out_specs=(vmem, vmem),
        scratch_shapes=[
            pltpu.VMEM((chips, 2, 2 * occ, virtual), jnp.bfloat16),
            pltpu.VMEM((chips, 2, 2 * occ, virtual), jnp.bfloat16),
            pltpu.VMEM((chips // depth, depth, 2, 1, rows), jnp.int32),
            pltpu.SemaphoreType.DMA((4,)),
            pltpu.SemaphoreType.DMA((6,)),
        ],
        compiler_params=pltpu.CompilerParams(
            collective_id=0, has_side_effects=True, vmem_limit_bytes=32 * 2**20
        ),
        name="route",
    )(row_target.reshape(1, rows), outgoing)

    ids = ids.reshape(devices, rows)
    mine = (ids // rows) == lax.axis_index("blk")
    earlier = (row_ids[:, None] < row_ids[None, :]).astype(jnp.bfloat16)
    order = jnp.dot(mine.astype(jnp.bfloat16), earlier, preferred_element_type=jnp.float32)
    place = lax.rem(ids, rows) + 1
    landing = jnp.stack(
        [jnp.sum(jnp.where(mine & (order == k), place, 0), axis=1) for k in range(2)], axis=1
    ).reshape(2 * devices)
    put = (row_ids[:, None] + 1 == landing[None, :]).astype(jnp.bfloat16)
    own = jnp.dot(
        put, got.reshape(2 * devices, width), preferred_element_type=jnp.float32
    ).astype(jnp.bfloat16)

    frequency = 0.5 * jnp.tan(jnp.pi * (freq_pick.astype(jnp.float32) + 0.5) / (2.0 * GRID))
    own_occ = lax.dynamic_slice_in_dim(occ_energy, lax.axis_index("pair") * occ, occ)
    factor = response_factor(own_occ, vir_energy, frequency)

    return pl.pallas_call(
        functools.partial(band_kernel, chips),
        out_shape=jax.ShapeDtypeStruct((freqs, rows, 2 * rows), jnp.float32),
        in_specs=[vmem, vmem],
        out_specs=vmem,
        scratch_shapes=[
            pltpu.VMEM((9, rows, width), jnp.bfloat16),
            pltpu.VMEM((freqs * rows, width), jnp.bfloat16),
            pltpu.VMEM((2, freqs * rows, rows), jnp.float32),
            pltpu.VMEM((STEPS, freqs * rows, rows), jnp.bfloat16),
            pltpu.VMEM((4, 2, freqs * rows, rows), jnp.bfloat16),
            pltpu.SemaphoreType.DMA((4,)),
            pltpu.SemaphoreType.DMA((4,)),
            pltpu.SemaphoreType.DMA((4,)),
            pltpu.SemaphoreType.DMA((4,)),
            pltpu.SemaphoreType.DMA((STEPS,)),
            pltpu.SemaphoreType.DMA((4, 2)),
        ],
        compiler_params=pltpu.CompilerParams(
            collective_id=1, has_side_effects=True, vmem_limit_bytes=48 * 2**20
        ),
        name="band",
    )(own, factor)


def solution(mesh):
    return jax.shard_map(
        shards,
        mesh=mesh,
        in_specs=(P("blk", "pair", None), P("blk"), P(), P(), P(), P()),
        out_specs=P(None, "blk", "pair"),
        check_vma=False,
    )
```

```python
import functools

import jax
import jax.numpy as jnp
from jax import lax
from jax.experimental import pallas as pl
from jax.experimental.pallas import tpu as pltpu
from jax.sharding import PartitionSpec as P

MESH = pl.DeviceIdType.MESH
GRID = 32
STEPS = 8


def route_kernel(chips, depth, ids_ref, out_ref, got_ref, all_ids_ref, staged, arrived, ids, pair_sem, sems):
    blk, pair = lax.axis_index("blk"), lax.axis_index("pair")
    chip, core = blk // 2, lax.rem(blk, 2)
    upper, low = chip // depth, lax.rem(chip, depth)
    uppers = chips // depth
    sibling = (chip * 2 + 1 - core, pair)

    def same_core(other):
        return (other * 2 + core, pair)

    barrier = pltpu.get_barrier_semaphore()
    pl.semaphore_signal(barrier, inc=1, device_id=sibling, device_id_type=MESH)

    def greet(i, carry):
        pl.semaphore_signal(
            barrier, inc=1, device_id=same_core(lax.rem(chip + i, chips)), device_id_type=MESH
        )
        return carry

    lax.fori_loop(1, chips, greet, 0)
    pl.semaphore_wait(barrier, chips)

    ids[upper, low, core] = ids_ref[...]
    swap_ids = pltpu.make_async_remote_copy(
        ids.at[upper, low, core],
        ids.at[upper, low, core],
        pair_sem.at[0],
        pair_sem.at[1],
        device_id=sibling,
        device_id_type=MESH,
    )
    swap_ids.start()
    swap = pltpu.make_async_remote_copy(
        out_ref.at[1 - core],
        staged.at[:, core],
        pair_sem.at[2],
        pair_sem.at[3],
        device_id=sibling,
        device_id_type=MESH,
    )
    swap.start()
    staged[:, core] = out_ref[core]
    swap_ids.wait()
    for i in range(1, depth):
        pltpu.make_async_remote_copy(
            ids.at[upper, low],
            ids.at[upper, low],
            sems.at[0],
            sems.at[1],
            device_id=same_core(upper * depth + lax.rem(low + i, depth)),
            device_id_type=MESH,
        ).start()
    swap.wait()

    def send(i, carry):
        other = lax.rem(chip + i * 27, chips)
        pltpu.make_async_remote_copy(
            staged.at[other],
            arrived.at[chip],
            sems.at[2],
            sems.at[3],
            device_id=same_core(other),
            device_id_type=MESH,
        ).start()
        return carry

    lax.fori_loop(1, chips, send, 0)
    arrived[chip] = staged[chip]
    low_part = ids.at[0, pl.ds(0, depth - 1)]
    pltpu.make_async_remote_copy(
        low_part, low_part, sems.at[0], sems.at[1], device_id=sibling, device_id_type=MESH
    ).wait()
    for i in range(1, uppers):
        pltpu.make_async_remote_copy(
            ids.at[upper],
            ids.at[upper],
            sems.at[4],
            sems.at[5],
            device_id=same_core(lax.rem(upper + i, uppers) * depth + low),
            device_id_type=MESH,
        ).start()
    upper_part = ids.at[pl.ds(0, uppers - 1)]
    pltpu.make_async_remote_copy(
        upper_part, upper_part, sems.at[4], sems.at[5], device_id=sibling, device_id_type=MESH
    ).wait()
    all_ids_ref[...] = ids[...]
    most = arrived.at[pl.ds(0, chips - 1)]
    pltpu.make_async_remote_copy(
        most, most, sems.at[2], sems.at[3], device_id=sibling, device_id_type=MESH
    ).wait()
    got_ref[...] = arrived[...]


def band_kernel(
    chips, depth, own_ref, factor_ref, result_ref, halo, weighted, partial, outbox, inbox,
    halo_send, halo_recv, core_send, core_recv, part_send, part_recv
):
    blk, pair = lax.axis_index("blk"), lax.axis_index("pair")
    pairs = 4
    chip, core = blk // 2, lax.rem(blk, 2)
    low = lax.rem(chip, depth)

    def along(by):
        return (lax.rem(chip + chips + by, chips) * 2 + core, pair)

    above, below = along(1), along(-1)
    sibling = (chip * 2 + 1 - core, pair)
    freqs = factor_ref.shape[0]
    rows = own_ref.shape[0]

    barrier = pltpu.get_barrier_semaphore()
    for other in (above, below, along(2), along(-2), sibling):
        pl.semaphore_signal(barrier, inc=1, device_id=other, device_id_type=MESH)
    for i in range(1, pairs):
        pl.semaphore_signal(
            barrier, inc=1, device_id=(blk, lax.rem(pair + i, pairs)), device_id_type=MESH
        )
    pl.semaphore_wait(barrier, 5 + pairs - 1)

    def link(source, slot, lane, other):
        return pltpu.make_async_remote_copy(
            source, halo.at[slot], halo_send.at[lane], halo_recv.at[lane], device_id=other, device_id_type=MESH
        )

    def across(source, slot, lane):
        return pltpu.make_async_remote_copy(
            source, halo.at[slot], core_send.at[lane], core_recv.at[lane], device_id=sibling, device_id_type=MESH
        )

    up = link(own_ref, 1 + core, 0, above)
    down = link(own_ref, 5 + core, 1, below)
    beside = across(own_ref, 3 + core, 0)
    def far(slot, lane, receive, other):
        return pltpu.make_async_remote_copy(
            own_ref, halo.at[slot], halo_send.at[lane], halo_recv.at[receive], device_id=other, device_id_type=MESH
        )

    far_down_own = far(7 + core, 4, 2, along(-2))
    far_up_own = far(0, 5, 3, along(2))
    serves_down, serves_up = low == 1, (low == depth - 2) & (core == 1)
    hands_down, hands_up = low != 0, (low != depth - 1) & (core == 1)
    down.start()
    up.start()
    beside.start()

    pl.when(serves_down)(far_down_own.start)

    pl.when(serves_up)(far_up_own.start)

    for k in range(freqs):
        weighted[pl.ds(k * rows, rows)] = (
            own_ref[...].astype(jnp.float32) * factor_ref[pl.ds(k, 1)]
        ).astype(jnp.bfloat16)

    def send_part(step, stop):
        return pltpu.make_async_remote_copy(
            outbox.at[step],
            inbox.at[pair, lax.rem(stop, 2)],
            part_send.at[step],
            part_recv.at[pair, lax.rem(stop, 2)],
            device_id=(blk, stop // 2),
            device_id_type=MESH,
        )

    def tile(step, stop, block):
        value = lax.dot_general(
            weighted[...], block, (((1,), (1,)), ((), ())), preferred_element_type=jnp.float32
        )

        @pl.when(stop // 2 == pair)
        def _():
            partial[lax.rem(stop, 2)] = value

        @pl.when(stop // 2 != pair)
        def _():
            outbox[step] = value.astype(jnp.bfloat16)
            send_part(step, stop).start()

    stops = (3, 4 - 2 * core, 1, 5, 2 - 2 * core, 6 - 2 * core, 6 * core, 7)
    tile(0, stops[0], own_ref[...])
    beside.wait_recv()
    tile(1, stops[1], halo[4 - core])
    down.wait_recv()
    down2 = link(halo.at[5 + core], 7 + core, 2, below)

    @pl.when(hands_down)
    def _():
        down2.start()

    cross_down = across(halo.at[5 + core], 5 + core, 1)
    cross_down.start()
    up.wait_recv()
    up2 = link(halo.at[2], 0, 3, above)

    @pl.when(hands_up)
    def _():
        up2.start()

    cross_up = across(halo.at[1 + core], 1 + core, 2)
    cross_up.start()
    tile(2, stops[2], halo[1 + core])
    tile(3, stops[3], halo[5 + core])
    cross_up.wait_recv()
    tile(4, stops[4], halo[2 - core])
    cross_down.wait_recv()
    tile(5, stops[5], halo[6 - core])
    last = across(halo.at[7 - 7 * core], 7 - 7 * core, 3)
    down2.wait_recv()

    @pl.when(core == 0)
    def _():
        last.start()

    tile(7, stops[7], halo[7 + core])

    @pl.when(core == 1)
    def _():
        up2.wait_recv()
        last.start()

    last.wait_recv()
    tile(6, stops[6], halo[7 * core])

    for copy in (up, down, beside, cross_up, cross_down, last):
        copy.wait_send()
    for taken, copy in (
        (hands_down, down2), (hands_up, up2), (serves_down, far_down_own), (serves_up, far_up_own)
    ):
        pl.when(taken)(copy.wait_send)

    for i in range(1, pairs):
        other = lax.rem(pair + i, pairs)
        for half in range(2):
            pltpu.make_async_remote_copy(
                outbox.at[0],
                inbox.at[other, half],
                part_send.at[0],
                part_recv.at[other, half],
                device_id=(blk, other),
                device_id_type=MESH,
            ).wait_recv()
    for step in range(STEPS):

        @pl.when(stops[step] // 2 != pair)
        def _():
            send_part(step, stops[step]).wait_send()

    scaling = 1.0 / 64.0
    for half in range(2):
        total = partial[half]
        for i in range(1, pairs):
            total = total + inbox[lax.rem(pair + i, pairs), half].astype(jnp.float32)
        result_ref[:, :, half * rows : (half + 1) * rows] = (total * scaling).reshape(freqs, rows, rows)


def response_factor(occ_values, vir_values, frequency):
    gap = vir_values[None, :] - occ_values[:, None]
    factor = 2.0 * gap[None] / (gap[None] * gap[None] + (frequency * frequency)[:, None, None])
    return factor.reshape(frequency.shape[0], -1)


def shards(half_blocks, row_target, vir_coeff, occ_energy, vir_energy, freq_pick):
    devices = lax.axis_size("blk")
    chips = devices // 2
    rows, occ, basis = half_blocks.shape
    virtual = vir_coeff.shape[1]
    width = occ * virtual
    freqs = freq_pick.shape[0]
    row_ids = jnp.arange(rows, dtype=jnp.int32)

    virt = jnp.dot(
        half_blocks.reshape(rows * occ, basis), vir_coeff, preferred_element_type=jnp.float32
    ).astype(jnp.bfloat16)
    owner = row_target // rows
    alike = owner[:, None] == owner[None, :]
    rank = jnp.sum((alike & (row_ids[None, :] < row_ids[:, None])).astype(jnp.int32), axis=1)
    slot = lax.rem(owner, 2) * devices + (owner // 2) * 2 + rank
    slots = jnp.arange(2 * devices, dtype=jnp.int32)
    pick = (slots[:, None] == slot[None, :]).astype(jnp.bfloat16)
    outgoing = jnp.dot(pick, virt.reshape(rows, width), preferred_element_type=jnp.float32)
    outgoing = outgoing.astype(jnp.bfloat16).reshape(2, chips, 2 * occ, virtual)

    depth = 8
    vmem = pl.BlockSpec(memory_space=pltpu.VMEM)
    got, ids = pl.pallas_call(
        functools.partial(route_kernel, chips, depth),
        out_shape=(
            jax.ShapeDtypeStruct((chips, 2, 2 * occ, virtual), jnp.bfloat16),
            jax.ShapeDtypeStruct((chips // depth, depth, 2, 1, rows), jnp.int32),
        ),
        in_specs=[vmem, vmem],
        out_specs=(vmem, vmem),
        scratch_shapes=[
            pltpu.VMEM((chips, 2, 2 * occ, virtual), jnp.bfloat16),
            pltpu.VMEM((chips, 2, 2 * occ, virtual), jnp.bfloat16),
            pltpu.VMEM((chips // depth, depth, 2, 1, rows), jnp.int32),
            pltpu.SemaphoreType.DMA((4,)),
            pltpu.SemaphoreType.DMA((6,)),
        ],
        compiler_params=pltpu.CompilerParams(
            collective_id=0, has_side_effects=True, vmem_limit_bytes=32 * 2**20
        ),
        name="route",
    )(row_target.reshape(1, rows), outgoing)

    ids = ids.reshape(devices, rows)
    mine = (ids // rows) == lax.axis_index("blk")
    earlier = (row_ids[:, None] < row_ids[None, :]).astype(jnp.bfloat16)
    order = jnp.dot(mine.astype(jnp.bfloat16), earlier, preferred_element_type=jnp.float32)
    place = lax.rem(ids, rows) + 1
    landing = jnp.stack(
        [jnp.sum(jnp.where(mine & (order == k), place, 0), axis=1) for k in range(2)], axis=1
    ).reshape(2 * devices)
    put = (row_ids[:, None] + 1 == landing[None, :]).astype(jnp.bfloat16)
    own = jnp.dot(
        put, got.reshape(2 * devices, width), preferred_element_type=jnp.float32
    ).astype(jnp.bfloat16)

    frequency = 0.5 * jnp.tan(jnp.pi * (freq_pick.astype(jnp.float32) + 0.5) / (2.0 * GRID))
    own_occ = lax.dynamic_slice_in_dim(occ_energy, lax.axis_index("pair") * occ, occ)
    factor = response_factor(own_occ, vir_energy, frequency)

    return pl.pallas_call(
        functools.partial(band_kernel, chips, depth),
        out_shape=jax.ShapeDtypeStruct((freqs, rows, 2 * rows), jnp.float32),
        in_specs=[vmem, vmem],
        out_specs=vmem,
        scratch_shapes=[
            pltpu.VMEM((9, rows, width), jnp.bfloat16),
            pltpu.VMEM((freqs * rows, width), jnp.bfloat16),
            pltpu.VMEM((2, freqs * rows, rows), jnp.float32),
            pltpu.VMEM((STEPS, freqs * rows, rows), jnp.bfloat16),
            pltpu.VMEM((4, 2, freqs * rows, rows), jnp.bfloat16),
            pltpu.SemaphoreType.DMA((6,)),
            pltpu.SemaphoreType.DMA((4,)),
            pltpu.SemaphoreType.DMA((4,)),
            pltpu.SemaphoreType.DMA((4,)),
            pltpu.SemaphoreType.DMA((STEPS,)),
            pltpu.SemaphoreType.DMA((4, 2)),
        ],
        compiler_params=pltpu.CompilerParams(
            collective_id=1, has_side_effects=True, vmem_limit_bytes=48 * 2**20
        ),
        name="band",
    )(own, factor)


def solution(mesh):
    return jax.shard_map(
        shards,
        mesh=mesh,
        in_specs=(P("blk", "pair", None), P("blk"), P(), P(), P(), P()),
        out_specs=P(None, "blk", "pair"),
        check_vma=False,
    )
```

```python
import functools

import jax
import jax.numpy as jnp
from jax import lax
from jax.experimental import pallas as pl
from jax.experimental.pallas import tpu as pltpu
from jax.sharding import PartitionSpec as P

MESH = pl.DeviceIdType.MESH
GRID = 32
STEPS = 8


def route_kernel(chips, depth, ids_ref, out_ref, got_ref, all_ids_ref, staged, arrived, ids, pair_sem, sems):
    blk, pair = lax.axis_index("blk"), lax.axis_index("pair")
    chip, core = blk // 2, lax.rem(blk, 2)
    upper, low = chip // depth, lax.rem(chip, depth)
    uppers = chips // depth
    sibling = (chip * 2 + 1 - core, pair)

    def same_core(other):
        return (other * 2 + core, pair)

    barrier = pltpu.get_barrier_semaphore()
    pl.semaphore_signal(barrier, inc=1, device_id=sibling, device_id_type=MESH)

    def greet(i, carry):
        pl.semaphore_signal(
            barrier, inc=1, device_id=same_core(lax.rem(chip + i, chips)), device_id_type=MESH
        )
        return carry

    lax.fori_loop(1, chips, greet, 0)
    pl.semaphore_wait(barrier, chips)

    ids[upper, low, core] = ids_ref[...]
    swap_ids = pltpu.make_async_remote_copy(
        ids.at[upper, low, core],
        ids.at[upper, low, core],
        pair_sem.at[0],
        pair_sem.at[1],
        device_id=sibling,
        device_id_type=MESH,
    )
    swap_ids.start()
    swap = pltpu.make_async_remote_copy(
        out_ref.at[1 - core],
        staged.at[:, core],
        pair_sem.at[2],
        pair_sem.at[3],
        device_id=sibling,
        device_id_type=MESH,
    )
    swap.start()
    staged[:, core] = out_ref[core]
    swap_ids.wait()
    for i in range(1, depth):
        pltpu.make_async_remote_copy(
            ids.at[upper, low],
            ids.at[upper, low],
            sems.at[0],
            sems.at[1],
            device_id=same_core(upper * depth + lax.rem(low + i, depth)),
            device_id_type=MESH,
        ).start()
    swap.wait()

    def send(i, carry):
        other = lax.rem(chip + i * 27, chips)
        pltpu.make_async_remote_copy(
            staged.at[other],
            arrived.at[chip],
            sems.at[2],
            sems.at[3],
            device_id=same_core(other),
            device_id_type=MESH,
        ).start()
        return carry

    lax.fori_loop(1, chips, send, 0)
    arrived[chip] = staged[chip]
    low_part = ids.at[0, pl.ds(0, depth - 1)]
    pltpu.make_async_remote_copy(
        low_part, low_part, sems.at[0], sems.at[1], device_id=sibling, device_id_type=MESH
    ).wait()
    for i in range(1, uppers):
        pltpu.make_async_remote_copy(
            ids.at[upper],
            ids.at[upper],
            sems.at[4],
            sems.at[5],
            device_id=same_core(lax.rem(upper + i, uppers) * depth + low),
            device_id_type=MESH,
        ).start()
    upper_part = ids.at[pl.ds(0, uppers - 1)]
    pltpu.make_async_remote_copy(
        upper_part, upper_part, sems.at[4], sems.at[5], device_id=sibling, device_id_type=MESH
    ).wait()
    all_ids_ref[...] = ids[...]
    most = arrived.at[pl.ds(0, chips - 1)]
    pltpu.make_async_remote_copy(
        most, most, sems.at[2], sems.at[3], device_id=sibling, device_id_type=MESH
    ).wait()
    got_ref[...] = arrived[...]


def band_kernel(
    chips, depth, own_ref, occ_ref, vir_ref, pick_ref, result_ref, halo, weighted, partial, outbox, inbox,
    joint, relayed, halo_send, halo_recv, core_send, core_recv, part_send, part_recv, relay_send, relay_recv
):
    blk, pair = lax.axis_index("blk"), lax.axis_index("pair")
    pairs = 4
    chip, core = blk // 2, lax.rem(blk, 2)
    low = lax.rem(chip, depth)

    def along(by):
        return (lax.rem(chip + chips + by, chips) * 2 + core, pair)

    above, below = along(1), along(-1)
    sibling = (chip * 2 + 1 - core, pair)
    freqs = pick_ref.shape[0]
    rows, width = own_ref.shape
    virtual = vir_ref.shape[1]
    occ = width // virtual

    barrier = pltpu.get_barrier_semaphore()
    for other in (above, below, along(2), along(-2), sibling):
        pl.semaphore_signal(barrier, inc=1, device_id=other, device_id_type=MESH)
    for i in range(1, pairs):
        pl.semaphore_signal(
            barrier, inc=1, device_id=(blk, lax.rem(pair + i, pairs)), device_id_type=MESH
        )
    def link(source, slot, lane, other):
        return pltpu.make_async_remote_copy(
            source, halo.at[slot], halo_send.at[lane], halo_recv.at[lane], device_id=other, device_id_type=MESH
        )

    def across(source, slot, lane):
        return pltpu.make_async_remote_copy(
            source, halo.at[slot], core_send.at[lane], core_recv.at[lane], device_id=sibling, device_id_type=MESH
        )

    up = link(own_ref, 1 + core, 0, above)
    down = link(own_ref, 5 + core, 1, below)
    beside = across(own_ref, 3 + core, 0)
    def far(slot, lane, receive, other):
        return pltpu.make_async_remote_copy(
            own_ref, halo.at[slot], halo_send.at[lane], halo_recv.at[receive], device_id=other, device_id_type=MESH
        )

    far_down_own = far(7 + core, 4, 2, along(-2))
    far_up_own = far(0, 5, 3, along(2))
    serves_down, serves_up = low == 1, (low == depth - 2) & (core == 1)
    hands_down, hands_up = low != 0, (low != depth - 1) & (core == 1)
    outer = (pair == 0) | (pair == pairs - 1)
    inner = jnp.logical_not(outer)
    beside_me, opposite = 1 + pair // 2, (pairs - 1 - pair) // 2

    def across_middle(stop):
        return stop // 4 == opposite

    def via(stop):
        return outer & across_middle(stop)

    def joins(stop):
        return inner & across_middle(stop)

    def direct(stop):
        return (stop // 2 != pair) & jnp.logical_not(across_middle(stop))

    def part(slot, stop):
        half = lax.rem(stop, 2)
        return pltpu.make_async_remote_copy(
            outbox.at[slot],
            inbox.at[pair, half],
            part_send.at[slot],
            part_recv.at[pair, half],
            device_id=(blk, stop // 2),
            device_id_type=MESH,
        )

    def send_part(step, stop):
        return part(step, stop)

    def send_joint(stop):
        return part(STEPS + lax.rem(stop, 4), stop)

    def send_on(step, stop):
        which = lax.rem(stop, 4)
        return pltpu.make_async_remote_copy(
            outbox.at[step],
            relayed.at[which],
            relay_send.at[which],
            relay_recv.at[which],
            device_id=(blk, beside_me),
            device_id_type=MESH,
        )

    def product(block):
        return lax.dot_general(
            weighted[...], block, (((1,), (1,)), ((), ())), preferred_element_type=jnp.float32
        )

    def keep(step, stop, value):
        half = lax.rem(stop, 2)

        @pl.when(stop // 2 == pair)
        def _():
            partial[half] = value

        @pl.when(joins(stop))
        def _():
            joint[lax.rem(stop, 4)] = value

        @pl.when(direct(stop) | via(stop))
        def _():
            outbox[step] = value.astype(jnp.bfloat16)

    def dispatch(step, stop):
        pl.when(direct(stop))(send_part(step, stop).start)
        pl.when(via(stop))(send_on(step, stop).start)

    def tile(step, stop, block):
        keep(step, stop, product(block))
        dispatch(step, stop)

    def tiles(steps, blocks):
        both = product(jnp.concatenate(blocks, axis=0))
        for n, step in enumerate(steps):
            keep(step, stops[step], both[:, n * rows : (n + 1) * rows])
            dispatch(step, stops[step])

    def join(step):
        stop = stops[step]
        which = lax.rem(stop, 4)

        @pl.when(joins(stop))
        def _():
            pltpu.make_async_remote_copy(
                outbox.at[0], relayed.at[which], relay_send.at[which], relay_recv.at[which],
                device_id=(blk, pairs - 1 - pair), device_id_type=MESH,
            ).wait_recv()
            outbox[STEPS + which] = (joint[which] + relayed[which].astype(jnp.float32)).astype(jnp.bfloat16)
            send_joint(stop).start()

    stops = (3, 4 - 2 * core, 1, 5, 2 - 2 * core, 6 - 2 * core, 6 * core, 7)
    for k in range(freqs):
        picked = jnp.full((1, virtual), pick_ref[k], jnp.int32).astype(jnp.float32)
        frequency = 0.5 * jnp.tan(jnp.pi * (picked + 0.5) / (2.0 * GRID))
        for i in range(occ):
            gap = vir_ref[...] - occ_ref[pair * occ + i]
            factor = 2.0 * gap / (gap * gap + frequency * frequency)
            lanes = slice(i * virtual, (i + 1) * virtual)
            weighted[k * rows : (k + 1) * rows, lanes] = (
                own_ref[:, lanes].astype(jnp.float32) * factor
            ).astype(jnp.bfloat16)
    keep(0, stops[0], product(own_ref[...]))
    pl.semaphore_wait(barrier, 5 + pairs - 1)
    down.start()
    up.start()
    beside.start()

    pl.when(serves_down)(far_down_own.start)

    pl.when(serves_up)(far_up_own.start)
    dispatch(0, stops[0])
    beside.wait_recv()
    tile(1, stops[1], halo[4 - core])
    down.wait_recv()
    down2 = link(halo.at[5 + core], 7 + core, 2, below)

    @pl.when(hands_down)
    def _():
        down2.start()

    cross_down = across(halo.at[5 + core], 5 + core, 1)
    cross_down.start()
    up.wait_recv()
    up2 = link(halo.at[2], 0, 3, above)

    @pl.when(hands_up)
    def _():
        up2.start()

    cross_up = across(halo.at[1 + core], 1 + core, 2)
    cross_up.start()
    tiles((3, 2), (halo[5 + core], halo[1 + core]))
    join(0)
    join(1)
    cross_up.wait_recv()
    cross_down.wait_recv()
    tiles((5, 4), (halo[6 - core], halo[2 - core]))
    last = across(halo.at[7 - 7 * core], 7 - 7 * core, 3)
    down2.wait_recv()

    @pl.when(core == 0)
    def _():
        last.start()

    tile(7, stops[7], halo[7 + core])

    @pl.when(core == 1)
    def _():
        up2.wait_recv()
        last.start()

    join(3)
    join(2)
    last.wait_recv()
    tile(6, stops[6], halo[7 * core])
    join(5)
    join(4)
    join(7)
    join(6)

    for copy in (up, down, beside, cross_up, cross_down, last):
        copy.wait_send()
    for taken, copy in (
        (hands_down, down2), (hands_up, up2), (serves_down, far_down_own), (serves_up, far_up_own)
    ):
        pl.when(taken)(copy.wait_send)

    scaling = 1.0 / 64.0

    def collect(hops):
        for i in hops:
            other = lax.rem(pair + i, pairs)
            for half in range(2):
                pltpu.make_async_remote_copy(
                    outbox.at[0],
                    inbox.at[other, half],
                    part_send.at[0],
                    part_recv.at[other, half],
                    device_id=(blk, other),
                    device_id_type=MESH,
                ).wait_recv()
        for half in range(2):
            total = partial[half]
            for i in hops:
                total = total + inbox[lax.rem(pair + i, pairs), half].astype(jnp.float32)
            result_ref[:, :, half * rows : (half + 1) * rows] = (total * scaling).reshape(freqs, rows, rows)

    @pl.when(outer)
    def _():
        collect((1 + pair // 3, 2 + pair // 3))

    @pl.when(inner)
    def _():
        collect((1, 3))

    for step in range(STEPS):
        pl.when(direct(stops[step]))(send_part(step, stops[step]).wait_send)
        pl.when(via(stops[step]))(send_on(step, stops[step]).wait_send)
        pl.when(joins(stops[step]))(send_joint(stops[step]).wait_send)


def shards(half_blocks, row_target, vir_coeff, occ_energy, vir_energy, freq_pick):
    devices = lax.axis_size("blk")
    chips = devices // 2
    rows, occ, basis = half_blocks.shape
    virtual = vir_coeff.shape[1]
    width = occ * virtual
    freqs = freq_pick.shape[0]
    row_ids = jnp.arange(rows, dtype=jnp.int32)

    virt = jnp.dot(
        half_blocks.reshape(rows * occ, basis), vir_coeff, preferred_element_type=jnp.float32
    ).astype(jnp.bfloat16)
    owner = row_target // rows
    alike = owner[:, None] == owner[None, :]
    rank = jnp.sum((alike & (row_ids[None, :] < row_ids[:, None])).astype(jnp.int32), axis=1)
    slot = lax.rem(owner, 2) * devices + (owner // 2) * 2 + rank
    slots = jnp.arange(2 * devices, dtype=jnp.int32)
    pick = (slots[:, None] == slot[None, :]).astype(jnp.bfloat16)
    outgoing = jnp.dot(pick, virt.reshape(rows, width), preferred_element_type=jnp.float32)
    outgoing = outgoing.astype(jnp.bfloat16).reshape(2, chips, 2 * occ, virtual)

    depth = 8
    vmem = pl.BlockSpec(memory_space=pltpu.VMEM)
    got, ids = pl.pallas_call(
        functools.partial(route_kernel, chips, depth),
        out_shape=(
            jax.ShapeDtypeStruct((chips, 2, 2 * occ, virtual), jnp.bfloat16),
            jax.ShapeDtypeStruct((chips // depth, depth, 2, 1, rows), jnp.int32),
        ),
        in_specs=[vmem, vmem],
        out_specs=(vmem, vmem),
        scratch_shapes=[
            pltpu.VMEM((chips, 2, 2 * occ, virtual), jnp.bfloat16),
            pltpu.VMEM((chips, 2, 2 * occ, virtual), jnp.bfloat16),
            pltpu.VMEM((chips // depth, depth, 2, 1, rows), jnp.int32),
            pltpu.SemaphoreType.DMA((4,)),
            pltpu.SemaphoreType.DMA((6,)),
        ],
        compiler_params=pltpu.CompilerParams(
            collective_id=0, has_side_effects=True, vmem_limit_bytes=32 * 2**20
        ),
        name="route",
    )(row_target.reshape(1, rows), outgoing)

    ids = ids.reshape(devices, rows)
    mine = (ids // rows) == lax.axis_index("blk")
    earlier = (row_ids[:, None] < row_ids[None, :]).astype(jnp.bfloat16)
    order = jnp.dot(mine.astype(jnp.bfloat16), earlier, preferred_element_type=jnp.float32)
    place = lax.rem(ids, rows) + 1
    landing = jnp.stack(
        [jnp.sum(jnp.where(mine & (order == k), place, 0), axis=1) for k in range(2)], axis=1
    ).reshape(2 * devices)
    put = (row_ids[:, None] + 1 == landing[None, :]).astype(jnp.bfloat16)
    own = jnp.dot(
        put, got.reshape(2 * devices, width), preferred_element_type=jnp.float32
    ).astype(jnp.bfloat16)

    smem = pl.BlockSpec(memory_space=pltpu.SMEM)
    return pl.pallas_call(
        functools.partial(band_kernel, chips, depth),
        out_shape=jax.ShapeDtypeStruct((freqs, rows, 2 * rows), jnp.float32),
        in_specs=[vmem, smem, vmem, smem],
        out_specs=vmem,
        scratch_shapes=[
            pltpu.VMEM((9, rows, width), jnp.bfloat16),
            pltpu.VMEM((freqs * rows, width), jnp.bfloat16),
            pltpu.VMEM((2, freqs * rows, rows), jnp.float32),
            pltpu.VMEM((STEPS + 4, freqs * rows, rows), jnp.bfloat16),
            pltpu.VMEM((4, 2, freqs * rows, rows), jnp.bfloat16),
            pltpu.VMEM((4, freqs * rows, rows), jnp.float32),
            pltpu.VMEM((4, freqs * rows, rows), jnp.bfloat16),
            pltpu.SemaphoreType.DMA((6,)),
            pltpu.SemaphoreType.DMA((4,)),
            pltpu.SemaphoreType.DMA((4,)),
            pltpu.SemaphoreType.DMA((4,)),
            pltpu.SemaphoreType.DMA((STEPS + 4,)),
            pltpu.SemaphoreType.DMA((4, 2)),
            pltpu.SemaphoreType.DMA((4,)),
            pltpu.SemaphoreType.DMA((4,)),
        ],
        compiler_params=pltpu.CompilerParams(
            collective_id=1, has_side_effects=True, vmem_limit_bytes=48 * 2**20
        ),
        name="band",
    )(own, occ_energy, vir_energy.reshape(1, virtual), freq_pick)


def solution(mesh):
    return jax.shard_map(
        shards,
        mesh=mesh,
        in_specs=(P("blk", "pair", None), P("blk"), P(), P(), P(), P()),
        out_specs=P(None, "blk", "pair"),
        check_vma=False,
    )
```

```python
import functools

import jax
import jax.numpy as jnp
from jax import lax
from jax.experimental import pallas as pl
from jax.experimental.pallas import tpu as pltpu
from jax.sharding import PartitionSpec as P

MESH = pl.DeviceIdType.MESH
GRID = 32
STEPS = 8


def route_kernel(chips, depth, ids_ref, out_ref, got_ref, all_ids_ref, staged, arrived, ids, pair_sem, sems):
    blk, pair = lax.axis_index("blk"), lax.axis_index("pair")
    chip, core = blk // 2, lax.rem(blk, 2)
    upper, low = chip // depth, lax.rem(chip, depth)
    uppers = chips // depth
    sibling = (chip * 2 + 1 - core, pair)

    def same_core(other):
        return (other * 2 + core, pair)

    barrier = pltpu.get_barrier_semaphore()
    pl.semaphore_signal(barrier, inc=1, device_id=sibling, device_id_type=MESH)

    def greet(i, carry):
        pl.semaphore_signal(
            barrier, inc=1, device_id=same_core(lax.rem(chip + i, chips)), device_id_type=MESH
        )
        return carry

    lax.fori_loop(1, chips, greet, 0)
    pl.semaphore_wait(barrier, chips)

    ids[upper, low, core] = ids_ref[...]
    swap_ids = pltpu.make_async_remote_copy(
        ids.at[upper, low, core],
        ids.at[upper, low, core],
        pair_sem.at[0],
        pair_sem.at[1],
        device_id=sibling,
        device_id_type=MESH,
    )
    swap_ids.start()
    swap = pltpu.make_async_remote_copy(
        out_ref.at[1 - core],
        staged.at[:, core],
        pair_sem.at[2],
        pair_sem.at[3],
        device_id=sibling,
        device_id_type=MESH,
    )
    swap.start()
    staged[:, core] = out_ref[core]
    swap_ids.wait()
    for i in range(1, depth):
        pltpu.make_async_remote_copy(
            ids.at[upper, low],
            ids.at[upper, low],
            sems.at[0],
            sems.at[1],
            device_id=same_core(upper * depth + lax.rem(low + i, depth)),
            device_id_type=MESH,
        ).start()
    swap.wait()

    def send(i, carry):
        other = lax.rem(chip + i * 27, chips)
        pltpu.make_async_remote_copy(
            staged.at[other],
            arrived.at[chip],
            sems.at[2],
            sems.at[3],
            device_id=same_core(other),
            device_id_type=MESH,
        ).start()
        return carry

    lax.fori_loop(1, chips, send, 0)
    arrived[chip] = staged[chip]
    low_part = ids.at[0, pl.ds(0, depth - 1)]
    pltpu.make_async_remote_copy(
        low_part, low_part, sems.at[0], sems.at[1], device_id=sibling, device_id_type=MESH
    ).wait()
    for i in range(1, uppers):
        pltpu.make_async_remote_copy(
            ids.at[upper],
            ids.at[upper],
            sems.at[4],
            sems.at[5],
            device_id=same_core(lax.rem(upper + i, uppers) * depth + low),
            device_id_type=MESH,
        ).start()
    upper_part = ids.at[pl.ds(0, uppers - 1)]
    pltpu.make_async_remote_copy(
        upper_part, upper_part, sems.at[4], sems.at[5], device_id=sibling, device_id_type=MESH
    ).wait()
    all_ids_ref[...] = ids[...]
    most = arrived.at[pl.ds(0, chips - 1)]
    pltpu.make_async_remote_copy(
        most, most, sems.at[2], sems.at[3], device_id=sibling, device_id_type=MESH
    ).wait()
    got_ref[...] = arrived[...]


def band_kernel(
    chips, depth, own_ref, occ_ref, vir_ref, pick_ref, result_ref, halo, weighted, partial, outbox, inbox,
    joint, relayed, halo_send, halo_recv, core_send, core_recv, part_send, part_recv, relay_send, relay_recv
):
    blk, pair = lax.axis_index("blk"), lax.axis_index("pair")
    pairs = 4
    chip, core = blk // 2, lax.rem(blk, 2)
    low = lax.rem(chip, depth)

    def along(by):
        return (lax.rem(chip + chips + by, chips) * 2 + core, pair)

    above, below = along(1), along(-1)
    sibling = (chip * 2 + 1 - core, pair)
    freqs = pick_ref.shape[0]
    rows, width = own_ref.shape
    virtual = vir_ref.shape[1]
    occ = width // virtual

    barrier = pltpu.get_barrier_semaphore()
    for other in (above, below, along(2), along(-2), along(3), along(-3), sibling):
        pl.semaphore_signal(barrier, inc=1, device_id=other, device_id_type=MESH)
    for i in range(1, pairs):
        pl.semaphore_signal(
            barrier, inc=1, device_id=(blk, lax.rem(pair + i, pairs)), device_id_type=MESH
        )
    def link(source, slot, lane, other):
        return pltpu.make_async_remote_copy(
            source, halo.at[slot], halo_send.at[lane], halo_recv.at[lane], device_id=other, device_id_type=MESH
        )

    def across(source, slot, lane):
        return pltpu.make_async_remote_copy(
            source, halo.at[slot], core_send.at[lane], core_recv.at[lane], device_id=sibling, device_id_type=MESH
        )

    up = link(own_ref, 1 + core, 0, above)
    down = link(own_ref, 5 + core, 1, below)
    beside = across(own_ref, 3 + core, 0)
    def far(source, target, lane, receive, by):
        return pltpu.make_async_remote_copy(
            source, target, halo_send.at[lane], halo_recv.at[receive], device_id=along(by), device_id_type=MESH
        )

    split = rows // 2
    first, second = pl.ds(0, split), pl.ds(split, rows - split)
    down_first = far(own_ref.at[first], halo.at[5 + core, first], 1, 1, -1)
    down_second = far(halo.at[1 + core, second], halo.at[5 + core, second], 6, 4, -2)
    far_down = far(halo.at[1 + core], halo.at[7 + core], 4, 2, -3)
    far_up_own = far(own_ref, halo.at[0], 5, 3, 2)
    lowest, highest = low == 0, low == depth - 1
    helps_down, serves_down = low == 1, low == 2
    serves_up = (low == depth - 2) & (core == 1)
    hands_down, hands_up = low != 0, (low != depth - 1) & (core == 1)
    outer = (pair == 0) | (pair == pairs - 1)
    inner = jnp.logical_not(outer)
    beside_me, opposite = 1 + pair // 2, (pairs - 1 - pair) // 2

    def across_middle(stop):
        return stop // 4 == opposite

    def via(stop):
        return outer & across_middle(stop)

    def joins(stop):
        return inner & across_middle(stop)

    def direct(stop):
        return (stop // 2 != pair) & jnp.logical_not(across_middle(stop))

    def part(slot, stop):
        half = lax.rem(stop, 2)
        return pltpu.make_async_remote_copy(
            outbox.at[slot],
            inbox.at[pair, half],
            part_send.at[slot],
            part_recv.at[pair, half],
            device_id=(blk, stop // 2),
            device_id_type=MESH,
        )

    def send_part(step, stop):
        return part(step, stop)

    def send_joint(stop):
        return part(STEPS + lax.rem(stop, 4), stop)

    def send_on(step, stop):
        which = lax.rem(stop, 4)
        return pltpu.make_async_remote_copy(
            outbox.at[step],
            relayed.at[which],
            relay_send.at[which],
            relay_recv.at[which],
            device_id=(blk, beside_me),
            device_id_type=MESH,
        )

    def product(block):
        return lax.dot_general(
            weighted[...], block, (((1,), (1,)), ((), ())), preferred_element_type=jnp.float32
        )

    def keep(step, stop, value):
        half = lax.rem(stop, 2)

        @pl.when(stop // 2 == pair)
        def _():
            partial[half] = value

        @pl.when(joins(stop))
        def _():
            joint[lax.rem(stop, 4)] = value

        @pl.when(direct(stop) | via(stop))
        def _():
            outbox[step] = value.astype(jnp.bfloat16)

    def dispatch(step, stop):
        pl.when(direct(stop))(send_part(step, stop).start)
        pl.when(via(stop))(send_on(step, stop).start)

    def tile(step, stop, block):
        keep(step, stop, product(block))
        dispatch(step, stop)

    def tiles(steps, blocks):
        both = product(jnp.concatenate(blocks, axis=0))
        for n, step in enumerate(steps):
            keep(step, stops[step], both[:, n * rows : (n + 1) * rows])
            dispatch(step, stops[step])

    def join(step):
        stop = stops[step]
        which = lax.rem(stop, 4)

        @pl.when(joins(stop))
        def _():
            pltpu.make_async_remote_copy(
                outbox.at[0], relayed.at[which], relay_send.at[which], relay_recv.at[which],
                device_id=(blk, pairs - 1 - pair), device_id_type=MESH,
            ).wait_recv()
            outbox[STEPS + which] = (joint[which] + relayed[which].astype(jnp.float32)).astype(jnp.bfloat16)
            send_joint(stop).start()

    stops = (3, 4 - 2 * core, 1, 5, 2 - 2 * core, 6 - 2 * core, 6 * core, 7)
    for k in range(freqs):
        picked = jnp.full((1, virtual), pick_ref[k], jnp.int32).astype(jnp.float32)
        frequency = 0.5 * jnp.tan(jnp.pi * (picked + 0.5) / (2.0 * GRID))
        for i in range(occ):
            gap = vir_ref[...] - occ_ref[pair * occ + i]
            factor = 2.0 * gap / (gap * gap + frequency * frequency)
            lanes = slice(i * virtual, (i + 1) * virtual)
            weighted[k * rows : (k + 1) * rows, lanes] = (
                own_ref[:, lanes].astype(jnp.float32) * factor
            ).astype(jnp.bfloat16)
    keep(0, stops[0], product(own_ref[...]))
    pl.semaphore_wait(barrier, 7 + pairs - 1)
    pl.when(lowest)(down_first.start)
    pl.when(jnp.logical_not(lowest))(down.start)
    up.start()
    beside.start()
    pl.when(serves_up)(far_up_own.start)
    dispatch(0, stops[0])
    beside.wait_recv()
    tile(1, stops[1], halo[4 - core])
    pl.when(jnp.logical_not(highest))(down.wait_recv)

    @pl.when(highest)
    def _():
        down_first.wait_recv()
        down_second.wait_recv()

    down2 = link(halo.at[5 + core], 7 + core, 2, below)

    @pl.when(hands_down)
    def _():
        down2.start()

    cross_down = across(halo.at[5 + core], 5 + core, 1)
    cross_down.start()
    up.wait_recv()
    pl.when(helps_down)(down_second.start)
    pl.when(serves_down)(far_down.start)
    up2 = link(halo.at[2], 0, 3, above)

    @pl.when(hands_up)
    def _():
        up2.start()

    cross_up = across(halo.at[1 + core], 1 + core, 2)
    cross_up.start()
    tiles((3, 2), (halo[5 + core], halo[1 + core]))
    join(0)
    join(1)
    cross_up.wait_recv()
    cross_down.wait_recv()
    tiles((5, 4), (halo[6 - core], halo[2 - core]))
    last = across(halo.at[7 - 7 * core], 7 - 7 * core, 3)
    down2.wait_recv()

    @pl.when(core == 0)
    def _():
        last.start()

    tile(7, stops[7], halo[7 + core])

    @pl.when(core == 1)
    def _():
        up2.wait_recv()
        last.start()

    join(3)
    join(2)
    last.wait_recv()
    tile(6, stops[6], halo[7 * core])
    join(5)
    join(4)
    join(7)
    join(6)

    for copy in (up, beside, cross_up, cross_down, last):
        copy.wait_send()
    for taken, copy in (
        (lowest, down_first), (jnp.logical_not(lowest), down), (helps_down, down_second),
        (hands_down, down2), (hands_up, up2), (serves_down, far_down), (serves_up, far_up_own)
    ):
        pl.when(taken)(copy.wait_send)

    scaling = 1.0 / 64.0

    def collect(hops):
        for i in hops:
            other = lax.rem(pair + i, pairs)
            for half in range(2):
                pltpu.make_async_remote_copy(
                    outbox.at[0],
                    inbox.at[other, half],
                    part_send.at[0],
                    part_recv.at[other, half],
                    device_id=(blk, other),
                    device_id_type=MESH,
                ).wait_recv()
        for half in range(2):
            total = partial[half]
            for i in hops:
                total = total + inbox[lax.rem(pair + i, pairs), half].astype(jnp.float32)
            result_ref[:, :, half * rows : (half + 1) * rows] = (total * scaling).reshape(freqs, rows, rows)

    @pl.when(outer)
    def _():
        collect((1 + pair // 3, 2 + pair // 3))

    @pl.when(inner)
    def _():
        collect((1, 3))

    for step in range(STEPS):
        pl.when(direct(stops[step]))(send_part(step, stops[step]).wait_send)
        pl.when(via(stops[step]))(send_on(step, stops[step]).wait_send)
        pl.when(joins(stops[step]))(send_joint(stops[step]).wait_send)


def shards(half_blocks, row_target, vir_coeff, occ_energy, vir_energy, freq_pick):
    devices = lax.axis_size("blk")
    chips = devices // 2
    rows, occ, basis = half_blocks.shape
    virtual = vir_coeff.shape[1]
    width = occ * virtual
    freqs = freq_pick.shape[0]
    row_ids = jnp.arange(rows, dtype=jnp.int32)

    virt = jnp.dot(
        half_blocks.reshape(rows * occ, basis), vir_coeff, preferred_element_type=jnp.float32
    ).astype(jnp.bfloat16)
    owner = row_target // rows
    alike = owner[:, None] == owner[None, :]
    rank = jnp.sum((alike & (row_ids[None, :] < row_ids[:, None])).astype(jnp.int32), axis=1)
    slot = lax.rem(owner, 2) * devices + (owner // 2) * 2 + rank
    slots = jnp.arange(2 * devices, dtype=jnp.int32)
    pick = (slots[:, None] == slot[None, :]).astype(jnp.bfloat16)
    outgoing = jnp.dot(pick, virt.reshape(rows, width), preferred_element_type=jnp.float32)
    outgoing = outgoing.astype(jnp.bfloat16).reshape(2, chips, 2 * occ, virtual)

    depth = 8
    vmem = pl.BlockSpec(memory_space=pltpu.VMEM)
    got, ids = pl.pallas_call(
        functools.partial(route_kernel, chips, depth),
        out_shape=(
            jax.ShapeDtypeStruct((chips, 2, 2 * occ, virtual), jnp.bfloat16),
            jax.ShapeDtypeStruct((chips // depth, depth, 2, 1, rows), jnp.int32),
        ),
        in_specs=[vmem, vmem],
        out_specs=(vmem, vmem),
        scratch_shapes=[
            pltpu.VMEM((chips, 2, 2 * occ, virtual), jnp.bfloat16),
            pltpu.VMEM((chips, 2, 2 * occ, virtual), jnp.bfloat16),
            pltpu.VMEM((chips // depth, depth, 2, 1, rows), jnp.int32),
            pltpu.SemaphoreType.DMA((4,)),
            pltpu.SemaphoreType.DMA((6,)),
        ],
        compiler_params=pltpu.CompilerParams(
            collective_id=0, has_side_effects=True, vmem_limit_bytes=32 * 2**20
        ),
        name="route",
    )(row_target.reshape(1, rows), outgoing)

    ids = ids.reshape(devices, rows)
    mine = (ids // rows) == lax.axis_index("blk")
    earlier = (row_ids[:, None] < row_ids[None, :]).astype(jnp.bfloat16)
    order = jnp.dot(mine.astype(jnp.bfloat16), earlier, preferred_element_type=jnp.float32)
    place = lax.rem(ids, rows) + 1
    landing = jnp.stack(
        [jnp.sum(jnp.where(mine & (order == k), place, 0), axis=1) for k in range(2)], axis=1
    ).reshape(2 * devices)
    put = (row_ids[:, None] + 1 == landing[None, :]).astype(jnp.bfloat16)
    own = jnp.dot(
        put, got.reshape(2 * devices, width), preferred_element_type=jnp.float32
    ).astype(jnp.bfloat16)

    smem = pl.BlockSpec(memory_space=pltpu.SMEM)
    return pl.pallas_call(
        functools.partial(band_kernel, chips, depth),
        out_shape=jax.ShapeDtypeStruct((freqs, rows, 2 * rows), jnp.float32),
        in_specs=[vmem, smem, vmem, smem],
        out_specs=vmem,
        scratch_shapes=[
            pltpu.VMEM((9, rows, width), jnp.bfloat16),
            pltpu.VMEM((freqs * rows, width), jnp.bfloat16),
            pltpu.VMEM((2, freqs * rows, rows), jnp.float32),
            pltpu.VMEM((STEPS + 4, freqs * rows, rows), jnp.bfloat16),
            pltpu.VMEM((4, 2, freqs * rows, rows), jnp.bfloat16),
            pltpu.VMEM((4, freqs * rows, rows), jnp.float32),
            pltpu.VMEM((4, freqs * rows, rows), jnp.bfloat16),
            pltpu.SemaphoreType.DMA((7,)),
            pltpu.SemaphoreType.DMA((5,)),
            pltpu.SemaphoreType.DMA((4,)),
            pltpu.SemaphoreType.DMA((4,)),
            pltpu.SemaphoreType.DMA((STEPS + 4,)),
            pltpu.SemaphoreType.DMA((4, 2)),
            pltpu.SemaphoreType.DMA((4,)),
            pltpu.SemaphoreType.DMA((4,)),
        ],
        compiler_params=pltpu.CompilerParams(
            collective_id=1, has_side_effects=True, vmem_limit_bytes=48 * 2**20
        ),
        name="band",
    )(own, occ_energy, vir_energy.reshape(1, virtual), freq_pick)


def solution(mesh):
    return jax.shard_map(
        shards,
        mesh=mesh,
        in_specs=(P("blk", "pair", None), P("blk"), P(), P(), P(), P()),
        out_specs=P(None, "blk", "pair"),
        check_vma=False,
    )
```

```python
import functools

import jax
import jax.numpy as jnp
from jax import lax
from jax.experimental import pallas as pl
from jax.experimental.pallas import tpu as pltpu
from jax.sharding import PartitionSpec as P

MESH = pl.DeviceIdType.MESH
GRID = 32
STEPS = 8


def route_kernel(chips, depth, ids_ref, out_ref, got_ref, all_ids_ref, staged, arrived, ids, pair_sem, sems):
    blk, pair = lax.axis_index("blk"), lax.axis_index("pair")
    chip, core = blk // 2, lax.rem(blk, 2)
    upper, low = chip // depth, lax.rem(chip, depth)
    uppers = chips // depth
    sibling = (chip * 2 + 1 - core, pair)

    def same_core(other):
        return (other * 2 + core, pair)

    barrier = pltpu.get_barrier_semaphore()
    pl.semaphore_signal(barrier, inc=1, device_id=sibling, device_id_type=MESH)

    def greet(i, carry):
        pl.semaphore_signal(
            barrier, inc=1, device_id=same_core(lax.rem(chip + i, chips)), device_id_type=MESH
        )
        return carry

    lax.fori_loop(1, chips, greet, 0)
    pl.semaphore_wait(barrier, chips)

    ids[upper, low, core] = ids_ref[...]
    swap_ids = pltpu.make_async_remote_copy(
        ids.at[upper, low, core],
        ids.at[upper, low, core],
        pair_sem.at[0],
        pair_sem.at[1],
        device_id=sibling,
        device_id_type=MESH,
    )
    swap_ids.start()
    swap = pltpu.make_async_remote_copy(
        out_ref.at[1 - core],
        staged.at[:, core],
        pair_sem.at[2],
        pair_sem.at[3],
        device_id=sibling,
        device_id_type=MESH,
    )
    swap.start()
    staged[:, core] = out_ref[core]
    swap_ids.wait()
    for i in range(1, depth):
        pltpu.make_async_remote_copy(
            ids.at[upper, low],
            ids.at[upper, low],
            sems.at[0],
            sems.at[1],
            device_id=same_core(upper * depth + lax.rem(low + i, depth)),
            device_id_type=MESH,
        ).start()
    swap.wait()

    def send(i, carry):
        other = lax.rem(chip + i * 27, chips)
        pltpu.make_async_remote_copy(
            staged.at[other],
            arrived.at[chip],
            sems.at[2],
            sems.at[3],
            device_id=same_core(other),
            device_id_type=MESH,
        ).start()
        return carry

    lax.fori_loop(1, chips, send, 0)
    arrived[chip] = staged[chip]
    low_part = ids.at[0, pl.ds(0, depth - 1)]
    pltpu.make_async_remote_copy(
        low_part, low_part, sems.at[0], sems.at[1], device_id=sibling, device_id_type=MESH
    ).wait()
    for i in range(1, uppers):
        pltpu.make_async_remote_copy(
            ids.at[upper],
            ids.at[upper],
            sems.at[4],
            sems.at[5],
            device_id=same_core(lax.rem(upper + i, uppers) * depth + low),
            device_id_type=MESH,
        ).start()
    upper_part = ids.at[pl.ds(0, uppers - 1)]
    pltpu.make_async_remote_copy(
        upper_part, upper_part, sems.at[4], sems.at[5], device_id=sibling, device_id_type=MESH
    ).wait()
    all_ids_ref[...] = ids[...]
    most = arrived.at[pl.ds(0, chips - 1)]
    pltpu.make_async_remote_copy(
        most, most, sems.at[2], sems.at[3], device_id=sibling, device_id_type=MESH
    ).wait()
    got_ref[...] = arrived[...]


def band_kernel(
    chips, depth, own_ref, occ_ref, vir_ref, pick_ref, result_ref, halo, weighted, partial, outbox, inbox,
    joint, relayed, halo_send, halo_recv, core_send, core_recv, part_send, part_recv, relay_send, relay_recv
):
    blk, pair = lax.axis_index("blk"), lax.axis_index("pair")
    pairs = 4
    chip, core = blk // 2, lax.rem(blk, 2)
    low = lax.rem(chip, depth)

    def along(by):
        return (lax.rem(chip + chips + by, chips) * 2 + core, pair)

    above, below = along(1), along(-1)
    sibling = (chip * 2 + 1 - core, pair)
    freqs = pick_ref.shape[0]
    rows, width = own_ref.shape
    virtual = vir_ref.shape[1]
    occ = width // virtual

    barrier = pltpu.get_barrier_semaphore()
    for other in (above, below, along(2), along(-2), along(3), along(-3), sibling):
        pl.semaphore_signal(barrier, inc=1, device_id=other, device_id_type=MESH)
    for i in range(1, pairs):
        pl.semaphore_signal(
            barrier, inc=1, device_id=(blk, lax.rem(pair + i, pairs)), device_id_type=MESH
        )
    def link(source, slot, lane, other):
        return pltpu.make_async_remote_copy(
            source, halo.at[slot], halo_send.at[lane], halo_recv.at[lane], device_id=other, device_id_type=MESH
        )

    def across(source, slot, lane):
        return pltpu.make_async_remote_copy(
            source, halo.at[slot], core_send.at[lane], core_recv.at[lane], device_id=sibling, device_id_type=MESH
        )

    up = link(own_ref, 1 + core, 0, above)
    down = link(own_ref, 5 + core, 1, below)
    beside = across(own_ref, 3 + core, 0)
    def far(source, target, lane, receive, by):
        return pltpu.make_async_remote_copy(
            source, target, halo_send.at[lane], halo_recv.at[receive], device_id=along(by), device_id_type=MESH
        )

    split = rows // 2
    first, second = pl.ds(0, split), pl.ds(split, rows - split)
    down_first = far(own_ref.at[first], halo.at[5 + core, first], 1, 1, -1)
    down_second = far(halo.at[1 + core, second], halo.at[5 + core, second], 6, 4, -2)
    share = rows // 4
    near_rows, rest_rows = pl.ds(0, share), pl.ds(share, rows - share)
    far_near = far(own_ref.at[near_rows], halo.at[7 + core, near_rows], 4, 2, -2)
    far_rest = far(halo.at[1 + core, rest_rows], halo.at[7 + core, rest_rows], 4, 5, -3)
    far_up_own = far(own_ref, halo.at[0], 5, 3, 2)
    lowest, highest = low == 0, low == depth - 1
    helps_down, serves_down = low == 1, low == 2
    serves_up = (low == depth - 2) & (core == 1)
    hands_down, hands_up = low != 0, (low != depth - 1) & (core == 1)
    outer = (pair == 0) | (pair == pairs - 1)
    inner = jnp.logical_not(outer)
    beside_me, opposite = 1 + pair // 2, (pairs - 1 - pair) // 2

    def across_middle(stop):
        return stop // 4 == opposite

    def via(stop):
        return outer & across_middle(stop)

    def joins(stop):
        return inner & across_middle(stop)

    def direct(stop):
        return (stop // 2 != pair) & jnp.logical_not(across_middle(stop))

    def part(slot, stop):
        half = lax.rem(stop, 2)
        return pltpu.make_async_remote_copy(
            outbox.at[slot],
            inbox.at[pair, half],
            part_send.at[slot],
            part_recv.at[pair, half],
            device_id=(blk, stop // 2),
            device_id_type=MESH,
        )

    def send_part(step, stop):
        return part(step, stop)

    def send_joint(stop):
        return part(STEPS + lax.rem(stop, 4), stop)

    def send_on(step, stop):
        which = lax.rem(stop, 4)
        return pltpu.make_async_remote_copy(
            outbox.at[step],
            relayed.at[which],
            relay_send.at[which],
            relay_recv.at[which],
            device_id=(blk, beside_me),
            device_id_type=MESH,
        )

    def product(block):
        return lax.dot_general(
            weighted[...], block, (((1,), (1,)), ((), ())), preferred_element_type=jnp.float32
        )

    def keep(step, stop, value):
        half = lax.rem(stop, 2)

        @pl.when(stop // 2 == pair)
        def _():
            partial[half] = value

        @pl.when(joins(stop))
        def _():
            joint[lax.rem(stop, 4)] = value

        @pl.when(direct(stop) | via(stop))
        def _():
            outbox[step] = value.astype(jnp.bfloat16)

    def dispatch(step, stop):
        pl.when(direct(stop))(send_part(step, stop).start)
        pl.when(via(stop))(send_on(step, stop).start)

    def tile(step, stop, block):
        keep(step, stop, product(block))
        dispatch(step, stop)

    def tiles(steps, blocks):
        both = product(jnp.concatenate(blocks, axis=0))
        for n, step in enumerate(steps):
            keep(step, stops[step], both[:, n * rows : (n + 1) * rows])
            dispatch(step, stops[step])

    def join(step):
        stop = stops[step]
        which = lax.rem(stop, 4)

        @pl.when(joins(stop))
        def _():
            pltpu.make_async_remote_copy(
                outbox.at[0], relayed.at[which], relay_send.at[which], relay_recv.at[which],
                device_id=(blk, pairs - 1 - pair), device_id_type=MESH,
            ).wait_recv()
            outbox[STEPS + which] = (joint[which] + relayed[which].astype(jnp.float32)).astype(jnp.bfloat16)
            send_joint(stop).start()

    stops = (3, 4 - 2 * core, 1, 5, 2 - 2 * core, 6 - 2 * core, 6 * core, 7)
    for k in range(freqs):
        picked = jnp.full((1, virtual), pick_ref[k], jnp.int32).astype(jnp.float32)
        frequency = 0.5 * jnp.tan(jnp.pi * (picked + 0.5) / (2.0 * GRID))
        for i in range(occ):
            gap = vir_ref[...] - occ_ref[pair * occ + i]
            factor = 2.0 * gap / (gap * gap + frequency * frequency)
            lanes = slice(i * virtual, (i + 1) * virtual)
            weighted[k * rows : (k + 1) * rows, lanes] = (
                own_ref[:, lanes].astype(jnp.float32) * factor
            ).astype(jnp.bfloat16)
    keep(0, stops[0], product(own_ref[...]))
    pl.semaphore_wait(barrier, 7 + pairs - 1)
    pl.when(lowest)(down_first.start)
    pl.when(jnp.logical_not(lowest))(down.start)
    up.start()
    beside.start()
    pl.when(helps_down)(far_near.start)
    pl.when(serves_up)(far_up_own.start)
    dispatch(0, stops[0])
    beside.wait_recv()
    tile(1, stops[1], halo[4 - core])
    pl.when(jnp.logical_not(highest))(down.wait_recv)

    @pl.when(highest)
    def _():
        down_first.wait_recv()
        down_second.wait_recv()

    down2 = link(halo.at[5 + core], 7 + core, 2, below)

    @pl.when(hands_down)
    def _():
        down2.start()

    cross_down = across(halo.at[5 + core], 5 + core, 1)
    cross_down.start()
    up.wait_recv()
    pl.when(helps_down)(down_second.start)
    pl.when(serves_down)(far_rest.start)
    up2 = link(halo.at[2], 0, 3, above)

    @pl.when(hands_up)
    def _():
        up2.start()

    cross_up = across(halo.at[1 + core], 1 + core, 2)
    cross_up.start()
    tiles((3, 2), (halo[5 + core], halo[1 + core]))
    join(0)
    join(1)
    cross_up.wait_recv()
    cross_down.wait_recv()
    tiles((5, 4), (halo[6 - core], halo[2 - core]))
    last = across(halo.at[7 - 7 * core], 7 - 7 * core, 3)
    pl.when(jnp.logical_not(highest))(down2.wait_recv)

    @pl.when(highest)
    def _():
        far_near.wait_recv()
        far_rest.wait_recv()


    @pl.when(core == 0)
    def _():
        last.start()

    tile(7, stops[7], halo[7 + core])

    @pl.when(core == 1)
    def _():
        up2.wait_recv()
        last.start()

    join(3)
    join(2)
    last.wait_recv()
    tile(6, stops[6], halo[7 * core])
    join(5)
    join(4)
    join(7)
    join(6)

    for copy in (up, beside, cross_up, cross_down, last):
        copy.wait_send()
    for taken, copy in (
        (lowest, down_first), (jnp.logical_not(lowest), down), (helps_down, down_second),
        (hands_down, down2), (hands_up, up2), (helps_down, far_near), (serves_down, far_rest), (serves_up, far_up_own)
    ):
        pl.when(taken)(copy.wait_send)

    scaling = 1.0 / 64.0

    def collect(hops):
        for i in hops:
            other = lax.rem(pair + i, pairs)
            for half in range(2):
                pltpu.make_async_remote_copy(
                    outbox.at[0],
                    inbox.at[other, half],
                    part_send.at[0],
                    part_recv.at[other, half],
                    device_id=(blk, other),
                    device_id_type=MESH,
                ).wait_recv()
        for half in range(2):
            total = partial[half]
            for i in hops:
                total = total + inbox[lax.rem(pair + i, pairs), half].astype(jnp.float32)
            result_ref[:, :, half * rows : (half + 1) * rows] = (total * scaling).reshape(freqs, rows, rows)

    @pl.when(outer)
    def _():
        collect((1 + pair // 3, 2 + pair // 3))

    @pl.when(inner)
    def _():
        collect((1, 3))

    for step in range(STEPS):
        pl.when(direct(stops[step]))(send_part(step, stops[step]).wait_send)
        pl.when(via(stops[step]))(send_on(step, stops[step]).wait_send)
        pl.when(joins(stops[step]))(send_joint(stops[step]).wait_send)


def shards(half_blocks, row_target, vir_coeff, occ_energy, vir_energy, freq_pick):
    devices = lax.axis_size("blk")
    chips = devices // 2
    rows, occ, basis = half_blocks.shape
    virtual = vir_coeff.shape[1]
    width = occ * virtual
    freqs = freq_pick.shape[0]
    row_ids = jnp.arange(rows, dtype=jnp.int32)

    virt = jnp.dot(
        half_blocks.reshape(rows * occ, basis), vir_coeff, preferred_element_type=jnp.float32
    ).astype(jnp.bfloat16)
    owner = row_target // rows
    alike = owner[:, None] == owner[None, :]
    rank = jnp.sum((alike & (row_ids[None, :] < row_ids[:, None])).astype(jnp.int32), axis=1)
    slot = lax.rem(owner, 2) * devices + (owner // 2) * 2 + rank
    slots = jnp.arange(2 * devices, dtype=jnp.int32)
    pick = (slots[:, None] == slot[None, :]).astype(jnp.bfloat16)
    outgoing = jnp.dot(pick, virt.reshape(rows, width), preferred_element_type=jnp.float32)
    outgoing = outgoing.astype(jnp.bfloat16).reshape(2, chips, 2 * occ, virtual)

    depth = 8
    vmem = pl.BlockSpec(memory_space=pltpu.VMEM)
    got, ids = pl.pallas_call(
        functools.partial(route_kernel, chips, depth),
        out_shape=(
            jax.ShapeDtypeStruct((chips, 2, 2 * occ, virtual), jnp.bfloat16),
            jax.ShapeDtypeStruct((chips // depth, depth, 2, 1, rows), jnp.int32),
        ),
        in_specs=[vmem, vmem],
        out_specs=(vmem, vmem),
        scratch_shapes=[
            pltpu.VMEM((chips, 2, 2 * occ, virtual), jnp.bfloat16),
            pltpu.VMEM((chips, 2, 2 * occ, virtual), jnp.bfloat16),
            pltpu.VMEM((chips // depth, depth, 2, 1, rows), jnp.int32),
            pltpu.SemaphoreType.DMA((4,)),
            pltpu.SemaphoreType.DMA((6,)),
        ],
        compiler_params=pltpu.CompilerParams(
            collective_id=0, has_side_effects=True, vmem_limit_bytes=32 * 2**20
        ),
        name="route",
    )(row_target.reshape(1, rows), outgoing)

    ids = ids.reshape(devices, rows)
    mine = (ids // rows) == lax.axis_index("blk")
    earlier = (row_ids[:, None] < row_ids[None, :]).astype(jnp.bfloat16)
    order = jnp.dot(mine.astype(jnp.bfloat16), earlier, preferred_element_type=jnp.float32)
    place = lax.rem(ids, rows) + 1
    landing = jnp.stack(
        [jnp.sum(jnp.where(mine & (order == k), place, 0), axis=1) for k in range(2)], axis=1
    ).reshape(2 * devices)
    put = (row_ids[:, None] + 1 == landing[None, :]).astype(jnp.bfloat16)
    own = jnp.dot(
        put, got.reshape(2 * devices, width), preferred_element_type=jnp.float32
    ).astype(jnp.bfloat16)

    smem = pl.BlockSpec(memory_space=pltpu.SMEM)
    return pl.pallas_call(
        functools.partial(band_kernel, chips, depth),
        out_shape=jax.ShapeDtypeStruct((freqs, rows, 2 * rows), jnp.float32),
        in_specs=[vmem, smem, vmem, smem],
        out_specs=vmem,
        scratch_shapes=[
            pltpu.VMEM((9, rows, width), jnp.bfloat16),
            pltpu.VMEM((freqs * rows, width), jnp.bfloat16),
            pltpu.VMEM((2, freqs * rows, rows), jnp.float32),
            pltpu.VMEM((STEPS + 4, freqs * rows, rows), jnp.bfloat16),
            pltpu.VMEM((4, 2, freqs * rows, rows), jnp.bfloat16),
            pltpu.VMEM((4, freqs * rows, rows), jnp.float32),
            pltpu.VMEM((4, freqs * rows, rows), jnp.bfloat16),
            pltpu.SemaphoreType.DMA((7,)),
            pltpu.SemaphoreType.DMA((6,)),
            pltpu.SemaphoreType.DMA((4,)),
            pltpu.SemaphoreType.DMA((4,)),
            pltpu.SemaphoreType.DMA((STEPS + 4,)),
            pltpu.SemaphoreType.DMA((4, 2)),
            pltpu.SemaphoreType.DMA((4,)),
            pltpu.SemaphoreType.DMA((4,)),
        ],
        compiler_params=pltpu.CompilerParams(
            collective_id=1, has_side_effects=True, vmem_limit_bytes=48 * 2**20
        ),
        name="band",
    )(own, occ_energy, vir_energy.reshape(1, virtual), freq_pick)


def solution(mesh):
    return jax.shard_map(
        shards,
        mesh=mesh,
        in_specs=(P("blk", "pair", None), P("blk"), P(), P(), P(), P()),
        out_specs=P(None, "blk", "pair"),
        check_vma=False,
    )
```

```python
import functools

import jax
import jax.numpy as jnp
from jax import lax
from jax.experimental import pallas as pl
from jax.experimental.pallas import tpu as pltpu
from jax.sharding import PartitionSpec as P

MESH = pl.DeviceIdType.MESH
GRID = 32
STEPS = 8


def route_kernel(chips, depth, ids_ref, out_ref, got_ref, all_ids_ref, staged, arrived, ids, pair_sem, sems):
    blk, pair = lax.axis_index("blk"), lax.axis_index("pair")
    chip, core = blk // 2, lax.rem(blk, 2)
    upper, low = chip // depth, lax.rem(chip, depth)
    uppers = chips // depth
    sibling = (chip * 2 + 1 - core, pair)

    def same_core(other):
        return (other * 2 + core, pair)

    barrier = pltpu.get_barrier_semaphore()
    pl.semaphore_signal(barrier, inc=1, device_id=sibling, device_id_type=MESH)

    def greet(i, carry):
        pl.semaphore_signal(
            barrier, inc=1, device_id=same_core(lax.rem(chip + i, chips)), device_id_type=MESH
        )
        return carry

    lax.fori_loop(1, chips, greet, 0)
    ids[upper, low, core] = ids_ref[...]
    staged[:, core] = out_ref[core]
    pl.semaphore_wait(barrier, chips)

    swap_ids = pltpu.make_async_remote_copy(
        ids.at[upper, low, core],
        ids.at[upper, low, core],
        pair_sem.at[0],
        pair_sem.at[1],
        device_id=sibling,
        device_id_type=MESH,
    )
    swap_ids.start()
    swap = pltpu.make_async_remote_copy(
        out_ref.at[1 - core],
        staged.at[:, core],
        pair_sem.at[2],
        pair_sem.at[3],
        device_id=sibling,
        device_id_type=MESH,
    )
    swap.start()
    swap_ids.wait()
    for i in range(1, depth):
        pltpu.make_async_remote_copy(
            ids.at[upper, low],
            ids.at[upper, low],
            sems.at[0],
            sems.at[1],
            device_id=same_core(upper * depth + lax.rem(low + i, depth)),
            device_id_type=MESH,
        ).start()
    swap.wait()

    def send(i, carry):
        other = lax.rem(chip + i * 27, chips)
        pltpu.make_async_remote_copy(
            staged.at[other],
            arrived.at[chip],
            sems.at[2],
            sems.at[3],
            device_id=same_core(other),
            device_id_type=MESH,
        ).start()
        return carry

    lax.fori_loop(1, chips, send, 0)
    arrived[chip] = staged[chip]
    low_part = ids.at[0, pl.ds(0, depth - 1)]
    pltpu.make_async_remote_copy(
        low_part, low_part, sems.at[0], sems.at[1], device_id=sibling, device_id_type=MESH
    ).wait()
    for i in range(1, uppers):
        pltpu.make_async_remote_copy(
            ids.at[upper],
            ids.at[upper],
            sems.at[4],
            sems.at[5],
            device_id=same_core(lax.rem(upper + i, uppers) * depth + low),
            device_id_type=MESH,
        ).start()
    upper_part = ids.at[pl.ds(0, uppers - 1)]
    pltpu.make_async_remote_copy(
        upper_part, upper_part, sems.at[4], sems.at[5], device_id=sibling, device_id_type=MESH
    ).wait()
    all_ids_ref[...] = ids[...]
    most = arrived.at[pl.ds(0, chips - 1)]
    pltpu.make_async_remote_copy(
        most, most, sems.at[2], sems.at[3], device_id=sibling, device_id_type=MESH
    ).wait()
    got_ref[...] = arrived[...]


def band_kernel(
    chips, depth, own_ref, occ_ref, vir_ref, pick_ref, result_ref, halo, weighted, partial, outbox, inbox,
    joint, relayed, halo_send, halo_recv, core_send, core_recv, part_send, part_recv, relay_send, relay_recv
):
    blk, pair = lax.axis_index("blk"), lax.axis_index("pair")
    pairs = 4
    chip, core = blk // 2, lax.rem(blk, 2)
    low = lax.rem(chip, depth)

    def along(by):
        return (lax.rem(chip + chips + by, chips) * 2 + core, pair)

    above, below = along(1), along(-1)
    sibling = (chip * 2 + 1 - core, pair)
    freqs = pick_ref.shape[0]
    rows, width = own_ref.shape
    virtual = vir_ref.shape[1]
    occ = width // virtual

    barrier = pltpu.get_barrier_semaphore()
    for other in (above, below, along(2), along(-2), along(3), along(-3), sibling):
        pl.semaphore_signal(barrier, inc=1, device_id=other, device_id_type=MESH)
    for i in range(1, pairs):
        pl.semaphore_signal(
            barrier, inc=1, device_id=(blk, lax.rem(pair + i, pairs)), device_id_type=MESH
        )
    def link(source, slot, lane, other):
        return pltpu.make_async_remote_copy(
            source, halo.at[slot], halo_send.at[lane], halo_recv.at[lane], device_id=other, device_id_type=MESH
        )

    def across(source, slot, lane):
        return pltpu.make_async_remote_copy(
            source, halo.at[slot], core_send.at[lane], core_recv.at[lane], device_id=sibling, device_id_type=MESH
        )

    up = link(own_ref, 1 + core, 0, above)
    down = link(own_ref, 5 + core, 1, below)
    beside = across(own_ref, 3 + core, 0)
    def far(source, target, lane, receive, by):
        return pltpu.make_async_remote_copy(
            source, target, halo_send.at[lane], halo_recv.at[receive], device_id=along(by), device_id_type=MESH
        )

    split = rows // 2
    first, second = pl.ds(0, split), pl.ds(split, rows - split)
    down_first = far(own_ref.at[first], halo.at[5 + core, first], 1, 1, -1)
    down_second = far(halo.at[1 + core, second], halo.at[5 + core, second], 6, 4, -2)
    share = rows // 4
    near_rows, rest_rows = pl.ds(0, share), pl.ds(share, rows - share)
    far_near = far(own_ref.at[near_rows], halo.at[7 + core, near_rows], 4, 2, -2)
    far_rest = far(halo.at[1 + core, rest_rows], halo.at[7 + core, rest_rows], 4, 5, -3)
    far_up_own = far(own_ref, halo.at[0], 5, 3, 2)
    lowest, highest = low == 0, low == depth - 1
    helps_down, serves_down = low == 1, low == 2
    serves_up = (low == depth - 2) & (core == 1)
    hands_down, hands_up = low != 0, (low != depth - 1) & (core == 1)
    outer = (pair == 0) | (pair == pairs - 1)
    inner = jnp.logical_not(outer)
    beside_me, opposite = 1 + pair // 2, (pairs - 1 - pair) // 2

    def across_middle(stop):
        return stop // 4 == opposite

    def via(stop):
        return outer & across_middle(stop)

    def joins(stop):
        return inner & across_middle(stop)

    def direct(stop):
        return (stop // 2 != pair) & jnp.logical_not(across_middle(stop))

    def part(slot, stop):
        half = lax.rem(stop, 2)
        return pltpu.make_async_remote_copy(
            outbox.at[slot],
            inbox.at[pair, half],
            part_send.at[slot],
            part_recv.at[pair, half],
            device_id=(blk, stop // 2),
            device_id_type=MESH,
        )

    def send_part(step, stop):
        return part(step, stop)

    def send_joint(stop):
        return part(STEPS + lax.rem(stop, 4), stop)

    def send_on(step, stop):
        which = lax.rem(stop, 4)
        return pltpu.make_async_remote_copy(
            outbox.at[step],
            relayed.at[which],
            relay_send.at[which],
            relay_recv.at[which],
            device_id=(blk, beside_me),
            device_id_type=MESH,
        )

    def product(block):
        return lax.dot_general(
            weighted[...], block, (((1,), (1,)), ((), ())), preferred_element_type=jnp.float32
        )

    def keep(step, stop, value):
        half = lax.rem(stop, 2)

        @pl.when(stop // 2 == pair)
        def _():
            partial[half] = value

        @pl.when(joins(stop))
        def _():
            joint[lax.rem(stop, 4)] = value

        @pl.when(direct(stop) | via(stop))
        def _():
            outbox[step] = value.astype(jnp.bfloat16)

    def dispatch(step, stop):
        pl.when(direct(stop))(send_part(step, stop).start)
        pl.when(via(stop))(send_on(step, stop).start)

    def tile(step, stop, block):
        keep(step, stop, product(block))
        dispatch(step, stop)

    def tiles(steps, blocks):
        both = product(jnp.concatenate(blocks, axis=0))
        for n, step in enumerate(steps):
            keep(step, stops[step], both[:, n * rows : (n + 1) * rows])
            dispatch(step, stops[step])

    def join(step):
        stop = stops[step]
        which = lax.rem(stop, 4)

        @pl.when(joins(stop))
        def _():
            pltpu.make_async_remote_copy(
                outbox.at[0], relayed.at[which], relay_send.at[which], relay_recv.at[which],
                device_id=(blk, pairs - 1 - pair), device_id_type=MESH,
            ).wait_recv()
            outbox[STEPS + which] = (joint[which] + relayed[which].astype(jnp.float32)).astype(jnp.bfloat16)
            send_joint(stop).start()

    stops = (3, 4 - 2 * core, 1, 5, 2 - 2 * core, 6 - 2 * core, 6 * core, 7)
    for k in range(freqs):
        picked = jnp.full((1, virtual), pick_ref[k], jnp.int32).astype(jnp.float32)
        frequency = 0.5 * jnp.tan(jnp.pi * (picked + 0.5) / (2.0 * GRID))
        for i in range(occ):
            gap = vir_ref[...] - occ_ref[pair * occ + i]
            factor = 2.0 * gap / (gap * gap + frequency * frequency)
            lanes = slice(i * virtual, (i + 1) * virtual)
            weighted[k * rows : (k + 1) * rows, lanes] = (
                own_ref[:, lanes].astype(jnp.float32) * factor
            ).astype(jnp.bfloat16)
    keep(0, stops[0], product(own_ref[...]))
    pl.semaphore_wait(barrier, 7 + pairs - 1)
    pl.when(lowest)(down_first.start)
    pl.when(jnp.logical_not(lowest))(down.start)
    up.start()
    beside.start()
    pl.when(helps_down)(far_near.start)
    pl.when(serves_up)(far_up_own.start)
    dispatch(0, stops[0])
    beside.wait_recv()
    tile(1, stops[1], halo[4 - core])
    pl.when(jnp.logical_not(highest))(down.wait_recv)

    @pl.when(highest)
    def _():
        down_first.wait_recv()
        down_second.wait_recv()

    down2 = link(halo.at[5 + core], 7 + core, 2, below)

    @pl.when(hands_down)
    def _():
        down2.start()

    cross_down = across(halo.at[5 + core], 5 + core, 1)
    cross_down.start()
    up.wait_recv()
    pl.when(helps_down)(down_second.start)
    pl.when(serves_down)(far_rest.start)
    up2 = link(halo.at[2], 0, 3, above)

    @pl.when(hands_up)
    def _():
        up2.start()

    cross_up = across(halo.at[1 + core], 1 + core, 2)
    cross_up.start()
    tiles((3, 2), (halo[5 + core], halo[1 + core]))
    join(0)
    join(1)
    cross_up.wait_recv()
    cross_down.wait_recv()
    tiles((5, 4), (halo[6 - core], halo[2 - core]))
    last = across(halo.at[7 - 7 * core], 7 - 7 * core, 3)
    pl.when(jnp.logical_not(highest))(down2.wait_recv)

    @pl.when(highest)
    def _():
        far_near.wait_recv()
        far_rest.wait_recv()


    @pl.when(core == 0)
    def _():
        last.start()

    tile(7, stops[7], halo[7 + core])

    @pl.when(core == 1)
    def _():
        up2.wait_recv()
        last.start()

    join(3)
    join(2)
    last.wait_recv()
    tile(6, stops[6], halo[7 * core])
    join(5)
    join(4)
    join(7)
    join(6)

    for copy in (up, beside, cross_up, cross_down, last):
        copy.wait_send()
    for taken, copy in (
        (lowest, down_first), (jnp.logical_not(lowest), down), (helps_down, down_second),
        (hands_down, down2), (hands_up, up2), (helps_down, far_near), (serves_down, far_rest), (serves_up, far_up_own)
    ):
        pl.when(taken)(copy.wait_send)

    scaling = 1.0 / 64.0

    def collect(hops):
        for half in (1, 0):
            total = partial[half]
            for i in hops:
                other = lax.rem(pair + i, pairs)
                pltpu.make_async_remote_copy(
                    outbox.at[0],
                    inbox.at[other, half],
                    part_send.at[0],
                    part_recv.at[other, half],
                    device_id=(blk, other),
                    device_id_type=MESH,
                ).wait_recv()
            for i in hops:
                total = total + inbox[lax.rem(pair + i, pairs), half].astype(jnp.float32)
            result_ref[:, :, half * rows : (half + 1) * rows] = (total * scaling).reshape(freqs, rows, rows)

    @pl.when(outer)
    def _():
        collect((1 + pair // 3, 2 + pair // 3))

    @pl.when(inner)
    def _():
        collect((1, 3))

    for step in range(STEPS):
        pl.when(direct(stops[step]))(send_part(step, stops[step]).wait_send)
        pl.when(via(stops[step]))(send_on(step, stops[step]).wait_send)
        pl.when(joins(stops[step]))(send_joint(stops[step]).wait_send)


def shards(half_blocks, row_target, vir_coeff, occ_energy, vir_energy, freq_pick):
    devices = lax.axis_size("blk")
    chips = devices // 2
    rows, occ, basis = half_blocks.shape
    virtual = vir_coeff.shape[1]
    width = occ * virtual
    freqs = freq_pick.shape[0]
    row_ids = jnp.arange(rows, dtype=jnp.int32)

    virt = jnp.dot(
        half_blocks.reshape(rows * occ, basis), vir_coeff, preferred_element_type=jnp.float32
    ).astype(jnp.bfloat16)
    owner = row_target // rows
    alike = owner[:, None] == owner[None, :]
    rank = jnp.sum((alike & (row_ids[None, :] < row_ids[:, None])).astype(jnp.int32), axis=1)
    slot = lax.rem(owner, 2) * devices + (owner // 2) * 2 + rank
    slots = jnp.arange(2 * devices, dtype=jnp.int32)
    pick = (slots[:, None] == slot[None, :]).astype(jnp.bfloat16)
    outgoing = jnp.dot(pick, virt.reshape(rows, width), preferred_element_type=jnp.float32)
    outgoing = outgoing.astype(jnp.bfloat16).reshape(2, chips, 2 * occ, virtual)

    depth = 8
    vmem = pl.BlockSpec(memory_space=pltpu.VMEM)
    got, ids = pl.pallas_call(
        functools.partial(route_kernel, chips, depth),
        out_shape=(
            jax.ShapeDtypeStruct((chips, 2, 2 * occ, virtual), jnp.bfloat16),
            jax.ShapeDtypeStruct((chips // depth, depth, 2, 1, rows), jnp.int32),
        ),
        in_specs=[vmem, vmem],
        out_specs=(vmem, vmem),
        scratch_shapes=[
            pltpu.VMEM((chips, 2, 2 * occ, virtual), jnp.bfloat16),
            pltpu.VMEM((chips, 2, 2 * occ, virtual), jnp.bfloat16),
            pltpu.VMEM((chips // depth, depth, 2, 1, rows), jnp.int32),
            pltpu.SemaphoreType.DMA((4,)),
            pltpu.SemaphoreType.DMA((6,)),
        ],
        compiler_params=pltpu.CompilerParams(
            collective_id=0, has_side_effects=True, vmem_limit_bytes=32 * 2**20
        ),
        name="route",
    )(row_target.reshape(1, rows), outgoing)

    ids = ids.reshape(devices, rows)
    mine = (ids // rows) == lax.axis_index("blk")
    earlier = (row_ids[:, None] < row_ids[None, :]).astype(jnp.bfloat16)
    order = jnp.dot(mine.astype(jnp.bfloat16), earlier, preferred_element_type=jnp.float32)
    place = lax.rem(ids, rows) + 1
    landing = jnp.stack(
        [jnp.sum(jnp.where(mine & (order == k), place, 0), axis=1) for k in range(2)], axis=1
    ).reshape(2 * devices)
    put = (row_ids[:, None] + 1 == landing[None, :]).astype(jnp.bfloat16)
    own = jnp.dot(
        put, got.reshape(2 * devices, width), preferred_element_type=jnp.float32
    ).astype(jnp.bfloat16)

    smem = pl.BlockSpec(memory_space=pltpu.SMEM)
    return pl.pallas_call(
        functools.partial(band_kernel, chips, depth),
        out_shape=jax.ShapeDtypeStruct((freqs, rows, 2 * rows), jnp.float32),
        in_specs=[vmem, smem, vmem, smem],
        out_specs=vmem,
        scratch_shapes=[
            pltpu.VMEM((9, rows, width), jnp.bfloat16),
            pltpu.VMEM((freqs * rows, width), jnp.bfloat16),
            pltpu.VMEM((2, freqs * rows, rows), jnp.float32),
            pltpu.VMEM((STEPS + 4, freqs * rows, rows), jnp.bfloat16),
            pltpu.VMEM((4, 2, freqs * rows, rows), jnp.bfloat16),
            pltpu.VMEM((4, freqs * rows, rows), jnp.float32),
            pltpu.VMEM((4, freqs * rows, rows), jnp.bfloat16),
            pltpu.SemaphoreType.DMA((7,)),
            pltpu.SemaphoreType.DMA((6,)),
            pltpu.SemaphoreType.DMA((4,)),
            pltpu.SemaphoreType.DMA((4,)),
            pltpu.SemaphoreType.DMA((STEPS + 4,)),
            pltpu.SemaphoreType.DMA((4, 2)),
            pltpu.SemaphoreType.DMA((4,)),
            pltpu.SemaphoreType.DMA((4,)),
        ],
        compiler_params=pltpu.CompilerParams(
            collective_id=1, has_side_effects=True, vmem_limit_bytes=48 * 2**20
        ),
        name="band",
    )(own, occ_energy, vir_energy.reshape(1, virtual), freq_pick)


def solution(mesh):
    return jax.shard_map(
        shards,
        mesh=mesh,
        in_specs=(P("blk", "pair", None), P("blk"), P(), P(), P(), P()),
        out_specs=P(None, "blk", "pair"),
        check_vma=False,
    )
```
